256 devices in a mesh: freq: 8 (over x, core), aux: 32 (over y, z).
Axes of the slice: x: 4, y: 4, z: 8, core: 2. Of those that a mesh axis runs over, the one named last changes fastest.
Arguments:
- screened: bfloat16 [16, 4096, 4096], P('freq', 'aux'), may hold values from -0.09375 to 0.09375
- grid_weights: float32 [16], replicated, may hold values from 0.2 to 0.5
- greens: float32 [16, 16], replicated, may hold values from 0.2 to 2
- three_state: bfloat16 [4096, 16, 128], P('aux'), may hold values from -6 to 6
- three_orbital: bfloat16 [4096, 16, 512], P('aux'), may hold values from -0.0234375 to 0.0234375
- block_ids: int32 [64, 8], P('aux'), may hold values from 0 to 7, each once within a row
- block_counts: int32 [64], P('aux'), may hold values from 1 to 8
- owners: int32 [32], replicated, may hold values from 0 to 31, each once
Outputs:
- self_energy: float32 [16, 512, 128], P('freq', 'aux')
The draws below stay inside these ranges and needn't reach their ends.
Inputs may be any that keep to these rules, and one draw needn't show every extreme that they name: `block_ids`: each row lists all 8 orbital blocks once, in a drawn order. `owners`: each device of aux owns exactly one orbital row block.
All inputs are finite; a program needn't handle non-finite values.
Results may differ from the reference program's by a relative error of at most 0.011.
Values may be sent and summed in bfloat16 or wider, within the bound.
No kernel may reach another device: no remote copies, remote signals or barrier semaphores. Data moves between devices by JAX's collectives and lax.ppermute only.
A program may use at most 128 MiB of HBM per device.

```python
import math
import jax
import jax.numpy as jnp
from jax import lax

NF = 16
NO = 512
MS = 128
OB = 64
RB = 64
KS = 16
P_SIZE = 4096
SLOTS = 8
NPB = 64
N_AUX = 32


def set_ends(array, own_key, low, high):
    spot = [jax.random.randint(jax.random.fold_in(own_key, axis), (), 0, length) for axis, length in enumerate(array.shape)]
    widest = array.shape.index(max(array.shape))
    next_to = spot[:widest] + [(spot[widest] + 1) % array.shape[widest]] + spot[widest + 1:]
    return array.at[tuple(spot)].set(low).at[tuple(next_to)].set(high)


def block_levels(key, shape, split, smallest, top_value):
    def one(dim, parts):
        heights = jax.random.uniform(jax.random.fold_in(jax.random.fold_in(key, 6), dim), (parts,), jnp.float32, smallest / len(split), top_value / len(split))
        return jnp.repeat(jnp.exp(heights), shape[dim] // parts).reshape((-1,) + (1,) * (len(shape) - dim - 1))

    gain = one(*split[0])
    for cut in split[1:]:
        gain = gain * one(*cut)
    return gain


def centred(key, extent, spread, reach, pieces=(), held_as=jnp.bfloat16):
    gain = block_levels(key, extent, pieces, -0.22, 0.18) if pieces else 1.0
    entries = jax.random.normal(key, extent, jnp.float32) * spread * gain
    return jnp.minimum(jnp.maximum(entries, -reach), reach).astype(held_as)


def setup_inputs(seed: int = 0) -> dict:
    keys = jax.random.split(jax.random.key(seed), 9)
    screened = centred(keys[0], (NF, P_SIZE, P_SIZE), P_SIZE ** -0.5, 0.09375, ((0, 8), (1, 32)))
    grid_weights = jnp.clip(jax.random.uniform(keys[1], (NF,), jnp.float32, 0.2, 0.5), 0.2, 0.5)
    greens = jnp.clip(jnp.exp(jax.random.uniform(keys[2], (NF, KS), jnp.float32, math.log(0.2), math.log(2.0))), 0.2, 2.0)
    three_state = centred(keys[3], (P_SIZE, KS, MS), 1.0, 6.0, ((0, 32),))
    three_orbital = centred(keys[4], (P_SIZE, KS, NO), (P_SIZE * KS) ** -0.5, 0.0234375, ((0, 32),))
    block_ids = jax.vmap(lambda own: jax.random.permutation(own, SLOTS))(jax.random.split(keys[5], NPB)).reshape((NPB, SLOTS)).astype(jnp.int32)
    block_counts = set_ends(jax.random.randint(keys[6], (NPB,), 1, SLOTS + 1), jax.random.fold_in(keys[6], 1), 1, SLOTS).astype(jnp.int32)
    owners = jax.random.permutation(keys[7], N_AUX).astype(jnp.int32)
    return {"screened": screened, "grid_weights": grid_weights, "greens": greens, "three_state": three_state, "three_orbital": three_orbital, "block_ids": block_ids, "block_counts": block_counts, "owners": owners}


def cosine_table(grid_weights, count):
    steps_t = jnp.arange(count, dtype=jnp.float32)
    return grid_weights[None, :] * jnp.cos(jnp.pi * (steps_t[:, None] + 0.5) * steps_t[None, :] / count)


def reference(screened, grid_weights, greens, three_state, three_orbital, block_ids, block_counts, owners):
    table = cosine_table(grid_weights, NF)
    flat_state = three_state.reshape(P_SIZE, KS * MS).astype(jnp.float32)

    def one_time(weights_row):
        def accumulate(index, total):
            piece = lax.dynamic_index_in_dim(screened, index, 0, keepdims=False)
            return total + weights_row[index] * piece.astype(jnp.float32)

        screened_time = lax.fori_loop(0, NF, accumulate, jnp.zeros((P_SIZE, P_SIZE), jnp.float32))
        return jnp.dot(screened_time, flat_state, precision=lax.Precision.HIGHEST)

    contracted = lax.map(one_time, table)
    scaled = (contracted.reshape(NF, P_SIZE, KS, MS) * greens[:, None, :, None]).astype(jnp.bfloat16)
    slot_index = jnp.arange(SLOTS, dtype=jnp.int32)
    onehot = ((block_ids[:, :, None] == slot_index[None, None, :]) & (slot_index[None, :, None] < block_counts[:, None, None])).astype(jnp.bfloat16)
    values = three_orbital.reshape(NPB, RB, KS, SLOTS, OB)
    dense_orbital = jnp.einsum("bsn,brksc->brknc", onehot, values, preferred_element_type=jnp.float32)
    dense_orbital = dense_orbital.reshape(P_SIZE * KS, NO).astype(jnp.bfloat16)

    def one_sigma(scaled_t):
        return jnp.dot(dense_orbital.T, scaled_t.reshape(P_SIZE * KS, MS), preferred_element_type=jnp.float32)

    partial_value = lax.map(one_sigma, scaled)
    inverse = jnp.argsort(owners).astype(jnp.int32)
    partial_value = jnp.take(partial_value.reshape(NF, N_AUX, NO // N_AUX, MS), inverse, axis=1)
    return partial_value.reshape(NF, NO, MS)
```

```python
import functools

import jax
import jax.numpy as jnp
from jax import lax
from jax.experimental import pallas as pl
from jax.experimental.pallas import tpu as pltpu
from jax.sharding import PartitionSpec as P

BAND = 16


def cosine_table(grid_weights, count):
    steps_t = jnp.arange(count, dtype=jnp.float32)
    return grid_weights[None, :] * jnp.cos(
        jnp.pi * (steps_t[:, None] + 0.5) * steps_t[None, :] / count
    )


def chunk_kernel(has_total, *refs):
    if has_total:
        pieces_ref, mix_ref, state_ref, greens_ref, dense_ref, total_ref = refs[:6]
        out_ref, timed_ref, scaled_ref = refs[6:]
    else:
        pieces_ref, mix_ref, state_ref, greens_ref, dense_ref = refs[:5]
        out_ref, timed_ref, scaled_ref = refs[5:]
    sources, local, rows, width = pieces_ref.shape
    freqs = sources * local
    times = greens_ref.shape[0]
    bands = rows // BAND
    targets = scaled_ref.shape[1] // times
    tall = times * BAND
    for band in range(bands):
        piece = pieces_ref[:, :, band * BAND : (band + 1) * BAND, :].reshape(freqs * BAND, width)
        mixed = jnp.dot(mix_ref[...], piece, preferred_element_type=jnp.float32)
        timed_ref[band * tall : (band + 1) * tall, :] = (mixed[:tall] + mixed[tall:]).astype(jnp.bfloat16)

    pair = 2 * targets

    def states(step, carry):
        columns = pl.ds(pl.multiple_of(step * pair, pair), pair)
        contracted = jnp.dot(timed_ref[...], state_ref[:, columns], preferred_element_type=jnp.float32)
        gains = greens_ref[:, columns]
        for time in range(times):
            gain = gains[time : time + 1, :]
            for band in range(bands):
                first = band * tall + time * BAND
                block = (contracted[first : first + BAND, :] * gain).astype(jnp.bfloat16)
                for state in range(2):
                    start = pl.multiple_of(step * 2 * rows + state * rows + band * BAND, BAND)
                    scaled_ref[pl.ds(start, BAND), time * targets : (time + 1) * targets] = block[
                        :, state * targets : (state + 1) * targets
                    ]
        return carry

    lax.fori_loop(0, state_ref.shape[1] // pair, states, 0)

    owners, inner = out_ref.shape[1], out_ref.shape[3]
    for place in range(times // 2):
        columns = slice(place * pair, (place + 1) * pair)
        value = jnp.dot(dense_ref[...], scaled_ref[:, columns], preferred_element_type=jnp.float32)
        for time in range(2):
            part = value[:, time * targets : (time + 1) * targets].reshape(owners, inner, targets)
            if has_total:
                part = part + total_ref[place, :, time, :, :]
            out_ref[place, :, time, :, :] = part.astype(out_ref.dtype)


def chunk(pieces, mix, state, gains, dense, total, owners, dtype):
    sources, local, rows, width = pieces.shape
    times = gains.shape[0]
    depth = dense.shape[1]
    targets = state.shape[1] * rows // depth
    shape = (times // 2, owners, 2, dense.shape[0] // owners, targets)
    operands = [pieces, mix, state, gains, dense]
    if total is not None:
        operands.append(total)
    return pl.pallas_call(
        functools.partial(chunk_kernel, total is not None),
        out_shape=jax.ShapeDtypeStruct(shape, dtype),
        in_specs=[pl.BlockSpec(memory_space=pltpu.VMEM)] * len(operands),
        out_specs=pl.BlockSpec(memory_space=pltpu.VMEM),
        scratch_shapes=[
            pltpu.VMEM((times * rows, width), jnp.bfloat16),
            pltpu.VMEM((depth, times * targets), jnp.bfloat16),
        ],
        compiler_params=pltpu.CompilerParams(vmem_limit_bytes=32 * 1024 * 1024),
        cost_estimate=pl.CostEstimate(
            flops=2 * times * rows * width * state.shape[1] + 2 * dense.shape[0] * depth * times * targets,
            bytes_accessed=8 * 1024 * 1024,
            transcendentals=0,
        ),
    )(*operands)


def shards(
    screened, grid_weights, greens, three_state, three_orbital, block_ids, block_counts, owners
):
    freq_count = lax.axis_size("freq")
    aux_count = lax.axis_size("aux")
    freq = lax.axis_index("freq")
    core = freq % 2
    local_times, rows, width = screened.shape
    total_times = local_times * freq_count
    states = three_state.shape[1]
    targets = three_state.shape[2]
    piece_width = width // freq_count
    block_count, slot_count = block_ids.shape
    orbitals = three_orbital.shape[2]
    block_width = orbitals // slot_count
    row_block = rows // block_count
    chips = freq_count // 2

    pieces = []
    for block in range(block_count):
        own = screened[:, block * row_block : (block + 1) * row_block, :]
        own = own.reshape(local_times, row_block, freq_count, piece_width).transpose(2, 0, 1, 3)
        pieces.append(lax.all_to_all(own, "freq", split_axis=0, concat_axis=0, tiled=True))

    share = rows // freq_count
    flat_state = three_state.reshape(rows, states * targets)
    own_state = lax.dynamic_slice_in_dim(flat_state, freq * share, share, 0)
    slabs = aux_count // freq_count
    moves = []
    for f in range(freq_count):
        for a in range(aux_count):
            moves.append(((a % freq_count) * aux_count + slabs * f + a // freq_count, f * aux_count + a))
    own_state = lax.ppermute(own_state, ("freq", "aux"), moves)
    state = lax.all_gather(own_state, "aux", axis=0, tiled=True)

    table = cosine_table(grid_weights, total_times)

    def halves(array):
        array = array.reshape(chips, 2, local_times, array.shape[1]).transpose(1, 0, 2, 3)
        array = array.reshape(2, chips * local_times, array.shape[3])
        return jnp.where(core == 0, array[::-1], array)

    table = halves(table)
    upper = table.astype(jnp.bfloat16)
    lower = (table - upper.astype(jnp.float32)).astype(jnp.bfloat16)
    same = jnp.eye(BAND, dtype=jnp.bfloat16)
    mix = jnp.stack([upper, lower], 1)
    mix = mix[:, :, :, None, :, None] * same[None, None, None, :, None, :]
    mix = mix.reshape(2, 2 * chips * local_times * BAND, total_times * BAND)
    gains = jnp.repeat(halves(greens), targets, axis=2)

    device = jnp.arange(aux_count, dtype=jnp.int32)
    owned = jnp.sum(jnp.where(owners[None, :] == device[:, None], device[None, :], 0), axis=1)
    inner = orbitals // aux_count
    wanted = (owned[:, None] * inner + jnp.arange(inner, dtype=jnp.int32)[None, :]).reshape(orbitals)
    slot = jnp.arange(slot_count, dtype=jnp.int32)
    listed = block_ids[:, :, None] * block_width + jnp.arange(block_width, dtype=jnp.int32)
    listed = jnp.where(slot[None, :, None] < block_counts[:, None, None], listed, -1).reshape(block_count, orbitals)
    choose = (wanted[None, :, None] == listed[:, None, :]).astype(jnp.bfloat16)
    values = three_orbital.reshape(block_count, row_block, states, orbitals)
    values = values.transpose(0, 2, 1, 3).reshape(block_count, states * row_block, orbitals)
    dense = jnp.einsum("bns,brs->bnr", choose, values, preferred_element_type=jnp.float32).astype(jnp.bfloat16)

    totals = [None, None]
    for block in range(block_count):
        last = block == block_count - 1
        for half in range(2):
            totals[half] = chunk(
                pieces[block], mix[half], state, gains[half], dense[block], totals[half], aux_count,
                jnp.bfloat16 if last and half == 0 else jnp.float32,
            )
    swap = [(f, f ^ 1) for f in range(freq_count)]
    other = lax.ppermute(totals[0], "freq", swap)
    summed = (totals[1] + other.astype(jnp.float32)).astype(jnp.bfloat16)
    groups = [[2 * chip + c for chip in range(chips)] for c in range(2)]
    spread = lax.all_to_all(
        summed, "freq", split_axis=0, concat_axis=0, axis_index_groups=groups, tiled=True
    )
    summed = jnp.sum(spread.astype(jnp.float32), axis=0).astype(jnp.bfloat16)
    spread = lax.all_to_all(summed, "aux", split_axis=0, concat_axis=0, tiled=True)
    return jnp.sum(spread.astype(jnp.float32), axis=0)


def solution(mesh):
    return jax.shard_map(
        shards,
        mesh=mesh,
        in_specs=(
            P("freq", "aux", None),
            P(),
            P(),
            P("aux", None, None),
            P("aux", None, None),
            P("aux", None),
            P("aux"),
            P(),
        ),
        out_specs=P("freq", "aux", None),
        check_vma=False,
    )
```

```python
import functools

import jax
import jax.numpy as jnp
from jax import lax
from jax.experimental import pallas as pl
from jax.experimental.pallas import tpu as pltpu
from jax.sharding import PartitionSpec as P

BAND = 16
DEPTH = 8
SHIFTS = ((0, 4, 3, 5, 2, 6, 1, 7), (0, 4, 1, 7, 2, 6, 3, 5))
WHOLE = pl.BlockSpec(memory_space=pltpu.VMEM)


def params():
    return pltpu.CompilerParams(vmem_limit_bytes=32 * 1024 * 1024)


def pick_kernel(place_ref, screened_ref, out_ref):
    place = place_ref[0]
    row, column = place // DEPTH, place % DEPTH
    odd = column % 2
    slab = out_ref.shape[3] // 4
    for f in range(out_ref.shape[0]):
        far = lax.rem(column + jnp.where(odd == 1, SHIFTS[1][f], SHIFTS[0][f]), DEPTH)
        for i in range(4):
            start = (lax.rem(row + i, 4) * DEPTH + far) * slab
            out_ref[f, :, :, i * slab : (i + 1) * slab] = screened_ref[:, :, pl.ds(pl.multiple_of(start, slab), slab)]


def pick(place, screened, freqs):
    local, rows, width = screened.shape
    tall = rows // 4
    return pl.pallas_call(
        pick_kernel,
        out_shape=jax.ShapeDtypeStruct((freqs, local, rows, width // freqs), screened.dtype),
        grid_spec=pltpu.PrefetchScalarGridSpec(
            num_scalar_prefetch=1,
            grid=(rows // tall,),
            in_specs=[pl.BlockSpec((local, tall, width), lambda i, place: (0, i, 0))],
            out_specs=pl.BlockSpec((freqs, local, tall, width // freqs), lambda i, place: (0, 0, i, 0)),
        ),
        compiler_params=params(),
    )(place, screened)


def mix_kernel(pieces_ref, mix_ref, out_ref):
    sources, local, rows, width = pieces_ref.shape
    freqs = sources * local
    tall = out_ref.shape[1] // (rows // BAND)
    for band in range(rows // BAND):
        piece = pieces_ref[:, :, band * BAND : (band + 1) * BAND, :].reshape(freqs * BAND, width)
        for half in range(2):
            mixed = jnp.dot(mix_ref[half], piece, preferred_element_type=jnp.float32)
            out_ref[half, band * tall : (band + 1) * tall, :] = (mixed[:tall] + mixed[tall:]).astype(jnp.bfloat16)


def transform(pieces, mix):
    sources, local, rows, width = pieces.shape
    times = sources * local // 2
    return pl.pallas_call(
        mix_kernel,
        out_shape=jax.ShapeDtypeStruct((2, times * rows, width), jnp.bfloat16),
        in_specs=[WHOLE] * 2,
        out_specs=WHOLE,
        compiler_params=params(),
    )(pieces, mix)


def contract_kernel(half, part, has_total, *refs):
    timed_ref, gains_ref, dense_ref = refs[:3]
    slabs = refs[3:7]
    refs = refs[7:]
    total_ref = None
    if has_total:
        total_ref, refs = refs[0], refs[1:]
    out_ref, state_ref, scaled_ref = refs
    slab = slabs[0].shape[0]
    for i in range(4):
        state_ref[i * slab : (i + 1) * slab, :] = slabs[i][...]
    times = gains_ref.shape[1]
    bands = timed_ref.shape[1] // (times * BAND)
    targets = scaled_ref.shape[1] // times
    span = state_ref.shape[1]
    blocks = dense_ref.shape[0]
    deep = scaled_ref.shape[0] // blocks
    bands_in = bands // blocks
    row_block = bands_in * BAND
    tall = times * BAND
    pair = 2 * targets

    def states(step, carry):
        columns = pl.ds(pl.multiple_of(step * pair, pair), pair)
        contracted = jnp.dot(timed_ref[half], state_ref[:, columns], preferred_element_type=jnp.float32)
        gains = gains_ref[half, :, pl.ds(pl.multiple_of(part * span + step * pair, pair), pair)]
        for time in range(times):
            gain = gains[time : time + 1, :]
            for band in range(bands):
                first = band * tall + time * BAND
                block = (contracted[first : first + BAND, :] * gain).astype(jnp.bfloat16)
                base = (band // bands_in) * deep + (band % bands_in) * BAND
                for state in range(2):
                    start = pl.multiple_of(base + (step * 2 + state) * row_block, BAND)
                    scaled_ref[pl.ds(start, BAND), time * targets : (time + 1) * targets] = block[
                        :, state * targets : (state + 1) * targets
                    ]
        return carry

    lax.fori_loop(0, span // pair, states, 0)

    owners, inner = out_ref.shape[1], out_ref.shape[3]
    for place in range(times // 2):
        columns = slice(place * pair, (place + 1) * pair)
        value = sum(
            jnp.dot(
                dense_ref[block, :, part * deep : (part + 1) * deep],
                scaled_ref[block * deep : (block + 1) * deep, columns],
                preferred_element_type=jnp.float32,
            )
            for block in range(blocks)
        )
        for time in range(2):
            piece = value[:, time * targets : (time + 1) * targets].reshape(owners, inner, targets)
            if has_total:
                piece = piece + total_ref[place, :, time, :, :]
            out_ref[place, :, time, :, :] = piece.astype(out_ref.dtype)


def contract(half, part, timed, gains, dense, slabs, total, owners, dtype):
    times = gains.shape[1]
    slab, span = slabs[0].shape
    rows = timed.shape[1] // times
    states = dense.shape[0] * dense.shape[2] // rows
    targets = gains.shape[2] // states
    depth = span // targets * rows
    shape = (times // 2, owners, 2, dense.shape[1] // owners, targets)
    operands = [timed, gains, dense, *slabs]
    if total is not None:
        operands.append(total)
    return pl.pallas_call(
        functools.partial(contract_kernel, half, part, total is not None),
        out_shape=jax.ShapeDtypeStruct(shape, dtype),
        in_specs=[WHOLE] * len(operands),
        out_specs=WHOLE,
        scratch_shapes=[
            pltpu.VMEM((4 * slab, span), jnp.bfloat16),
            pltpu.VMEM((depth, times * targets), jnp.bfloat16),
        ],
        compiler_params=params(),
        cost_estimate=pl.CostEstimate(
            flops=2 * timed.shape[1] * 4 * slab * span + 2 * dense.shape[1] * depth * times * targets,
            bytes_accessed=8 * 1024 * 1024,
            transcendentals=0,
        ),
    )(*operands)


def shards(
    screened, grid_weights, greens, three_state, three_orbital, block_ids, block_counts, owners
):
    freq_count = lax.axis_size("freq")
    aux_count = lax.axis_size("aux")
    freq = lax.axis_index("freq")
    chip, core = freq // 2, freq % 2
    local_times, rows, width = screened.shape
    total_times = local_times * freq_count
    states = three_state.shape[1]
    targets = three_state.shape[2]
    block_count, slot_count = block_ids.shape
    orbitals = three_orbital.shape[2]
    block_width = orbitals // slot_count
    row_block = rows // block_count
    chips = freq_count // 2
    height = aux_count // DEPTH

    along = []
    for f in range(freq_count):
        for y in range(height):
            for z in range(DEPTH):
                far = (z + SHIFTS[z % 2][f]) % DEPTH
                along.append((f * aux_count + y * DEPTH + far, f * aux_count + y * DEPTH + z))
    across = [
        [(((y + i) % height) * DEPTH + z, y * DEPTH + z) for y in range(height) for z in range(DEPTH)]
        for i in range(height)
    ]
    flat_state = three_state.reshape(rows, states * targets)
    span = states * targets // 2
    slabs = []
    for part in range(2):
        own = lax.ppermute(flat_state[:, part * span : (part + 1) * span], ("freq", "aux"), along)
        slabs.append([own] + [lax.ppermute(own, "aux", across[i]) for i in range(1, height)])

    place = lax.axis_index("aux").astype(jnp.int32).reshape(1)
    pieces = pick(place, screened, freq_count)
    pieces = lax.all_to_all(pieces, "freq", split_axis=0, concat_axis=0, tiled=True)

    half = jnp.arange(2, dtype=jnp.int32)[:, None, None]
    other = jnp.arange(chips, dtype=jnp.int32)[None, :, None]
    step = jnp.arange(local_times, dtype=jnp.int32)[None, None, :]
    time = ((chip + other) % chips) * 2 * local_times + ((core + 1 + half) % 2) * local_times + step
    time = time.reshape(2, chips * local_times)
    freqs = jnp.arange(total_times, dtype=jnp.int32)
    table = grid_weights * jnp.cos(
        jnp.pi * (time[:, :, None].astype(jnp.float32) + 0.5) * freqs.astype(jnp.float32) / total_times
    )
    upper = table.astype(jnp.bfloat16)
    lower = (table - upper.astype(jnp.float32)).astype(jnp.bfloat16)
    same = jnp.eye(BAND, dtype=jnp.bfloat16)
    mix = jnp.stack([upper, lower], 1)
    mix = mix[:, :, :, None, :, None] * same[None, None, None, :, None, :]
    mix = mix.reshape(2, 2 * chips * local_times * BAND, total_times * BAND)
    gains = jnp.sum(jnp.where(time[:, :, None, None] == freqs[:, None], greens, 0.0), axis=2)
    gains = jnp.repeat(gains, targets, axis=2)

    device = jnp.arange(aux_count, dtype=jnp.int32)
    owned = jnp.sum(jnp.where(owners[None, :] == device[:, None], device[None, :], 0), axis=1)
    inner = orbitals // aux_count
    wanted = (owned[:, None] * inner + jnp.arange(inner, dtype=jnp.int32)[None, :]).reshape(orbitals)
    slot = jnp.arange(slot_count, dtype=jnp.int32)
    listed = block_ids[:, :, None] * block_width + jnp.arange(block_width, dtype=jnp.int32)
    listed = jnp.where(slot[None, :, None] < block_counts[:, None, None], listed, -1).reshape(block_count, orbitals)
    choose = (wanted[None, :, None] == listed[:, None, :]).astype(jnp.bfloat16)
    values = three_orbital.reshape(block_count, row_block, states, orbitals)
    values = values.transpose(0, 2, 1, 3).reshape(block_count, states * row_block, orbitals)
    dense = jnp.einsum("bns,brs->bnr", choose, values, preferred_element_type=jnp.float32).astype(jnp.bfloat16)

    timed = transform(pieces, mix)
    partial = functools.partial(contract, timed=timed, gains=gains, dense=dense, owners=aux_count)
    given = partial(0, 0, slabs=slabs[0], total=None, dtype=jnp.float32)
    kept = partial(1, 0, slabs=slabs[0], total=None, dtype=jnp.float32)
    given = partial(0, 1, slabs=slabs[1], total=given, dtype=jnp.bfloat16)
    kept = partial(1, 1, slabs=slabs[1], total=kept, dtype=jnp.float32)
    taken = lax.ppermute(given, "freq", [(f, f ^ 1) for f in range(freq_count)])

    def chip_shift(by):
        return [(2 * x + c, 2 * ((x + by) % chips) + c) for x in range(chips) for c in range(2)]

    def joined(index):
        return kept[index] + taken[index].astype(jnp.float32)

    cut = aux_count // 2
    far = joined(2).astype(jnp.bfloat16)
    from_left = lax.ppermute(far[:cut], "freq", chip_shift(1))
    from_right = lax.ppermute(far[cut:], "freq", chip_shift(-1))
    right = joined(1).at[:cut].add(from_left.astype(jnp.float32)).astype(jnp.bfloat16)
    left = joined(3).at[cut:].add(from_right.astype(jnp.float32)).astype(jnp.bfloat16)
    from_left = lax.ppermute(right, "freq", chip_shift(1))
    from_right = lax.ppermute(left, "freq", chip_shift(-1))
    summed = joined(0) + from_left.astype(jnp.float32) + from_right.astype(jnp.float32)
    spread = lax.all_to_all(summed.astype(jnp.bfloat16), "aux", split_axis=0, concat_axis=0, tiled=True)
    return jnp.sum(spread.astype(jnp.float32), axis=0)


def solution(mesh):
    return jax.shard_map(
        shards,
        mesh=mesh,
        in_specs=(
            P("freq", "aux", None),
            P(),
            P(),
            P("aux", None, None),
            P("aux", None, None),
            P("aux", None),
            P("aux"),
            P(),
        ),
        out_specs=P("freq", "aux", None),
        check_vma=False,
    )
```

```python
import functools

import jax
import jax.numpy as jnp
from jax import lax
from jax.experimental import pallas as pl
from jax.experimental.pallas import tpu as pltpu
from jax.sharding import PartitionSpec as P

BAND = 16
DEPTH = 8
SHIFTS = ((0, 4, 3, 5, 2, 6, 1, 7), (0, 4, 1, 7, 2, 6, 3, 5))
WHOLE = pl.BlockSpec(memory_space=pltpu.VMEM)


def params():
    return pltpu.CompilerParams(vmem_limit_bytes=32 * 1024 * 1024)


def pick_kernel(place_ref, screened_ref, out_ref):
    place = place_ref[0]
    row, column = place // DEPTH, place % DEPTH
    odd = column % 2
    slab = out_ref.shape[3] // 4
    for f in range(out_ref.shape[0]):
        far = lax.rem(column + jnp.where(odd == 1, SHIFTS[1][f], SHIFTS[0][f]), DEPTH)
        for i in range(4):
            start = (lax.rem(row + i, 4) * DEPTH + far) * slab
            out_ref[f, :, :, i * slab : (i + 1) * slab] = screened_ref[:, :, pl.ds(pl.multiple_of(start, slab), slab)]


def pick(place, screened, freqs):
    local, rows, width = screened.shape
    tall = rows // 4
    return pl.pallas_call(
        pick_kernel,
        out_shape=jax.ShapeDtypeStruct((freqs, local, rows, width // freqs), screened.dtype),
        grid_spec=pltpu.PrefetchScalarGridSpec(
            num_scalar_prefetch=1,
            grid=(rows // tall,),
            in_specs=[pl.BlockSpec((local, tall, width), lambda i, place: (0, i, 0))],
            out_specs=pl.BlockSpec((freqs, local, tall, width // freqs), lambda i, place: (0, 0, i, 0)),
        ),
        compiler_params=params(),
    )(place, screened)


def mix_kernel(pieces_ref, table_ref, out_ref, mix_ref):
    sources, local, rows, width = pieces_ref.shape
    freqs = sources * local
    times = table_ref.shape[1]
    places = out_ref.shape[1]
    pair = 2 * BAND
    tall = times * BAND
    lane = lax.broadcasted_iota(jnp.int32, (BAND, freqs * BAND), 1) % BAND
    keep = lane == lax.broadcasted_iota(jnp.int32, (BAND, freqs * BAND), 0)
    for half in range(2):
        for time in range(times):
            value = jnp.where(keep, table_ref[half, time : time + 1, :], 0.0)
            upper = value.astype(jnp.bfloat16)
            lower = (value - upper.astype(jnp.float32)).astype(jnp.bfloat16)
            mix_ref[half, time * BAND : (time + 1) * BAND, :] = upper
            mix_ref[half, tall + time * BAND : tall + (time + 1) * BAND, :] = lower
    for band in range(rows // BAND):
        piece = pieces_ref[:, :, band * BAND : (band + 1) * BAND, :].reshape(freqs * BAND, width)
        for half in range(2):
            mixed = jnp.dot(mix_ref[half], piece, preferred_element_type=jnp.float32)
            mixed = (mixed[:tall] + mixed[tall:]).astype(jnp.bfloat16)
            for place in range(places):
                out_ref[half, place, band * pair : (band + 1) * pair, :] = mixed[place * pair : (place + 1) * pair]


def transform(pieces, table):
    sources, local, rows, width = pieces.shape
    freqs = sources * local
    times = table.shape[1]
    return pl.pallas_call(
        mix_kernel,
        out_shape=jax.ShapeDtypeStruct((2, times // 2, 2 * rows, width), jnp.bfloat16),
        in_specs=[WHOLE] * 2,
        out_specs=WHOLE,
        scratch_shapes=[pltpu.VMEM((2, 2 * times * BAND, freqs * BAND), jnp.bfloat16)],
        compiler_params=params(),
    )(pieces, table)


def contract_kernel(jobs, part, has_total, *refs):
    timed_ref, gains_ref, dense_ref = refs[:3]
    slabs = refs[3:7]
    refs = refs[7:]
    totals = [None] * len(jobs)
    if has_total:
        totals, refs = refs[: len(jobs)], refs[len(jobs) :]
    outs, (state_ref, scaled_ref) = refs[: len(jobs)], refs[len(jobs) :]
    slab = slabs[0].shape[0]
    for i in range(4):
        state_ref[i * slab : (i + 1) * slab, :] = slabs[i][...]
    span = state_ref.shape[1]
    blocks = dense_ref.shape[0]
    deep = scaled_ref.shape[0] // blocks
    tall, depth = timed_ref.shape[2:]
    bands = tall // (2 * BAND)
    bands_in = bands // blocks
    row_block = bands_in * BAND
    owners, inner, targets = outs[0].shape[1], outs[0].shape[3], outs[0].shape[4]
    pair = 2 * targets

    for (half, first, count), total_ref, out_ref in zip(jobs, totals, outs):
        timed = timed_ref[half, first : first + count].reshape(count * tall, depth)

        def states(step, carry):
            columns = pl.ds(pl.multiple_of(step * pair, pair), pair)
            contracted = jnp.dot(timed, state_ref[:, columns], preferred_element_type=jnp.float32)
            gains = gains_ref[half, :, pl.ds(pl.multiple_of(part * span + step * pair, pair), pair)]
            for place in range(count):
                for time in range(2):
                    at = 2 * (first + place) + time
                    gain = gains[at : at + 1, :]
                    column = (2 * place + time) * targets
                    for band in range(bands):
                        row = place * tall + (2 * band + time) * BAND
                        block = (contracted[row : row + BAND, :] * gain).astype(jnp.bfloat16)
                        base = (band // bands_in) * deep + (band % bands_in) * BAND
                        for state in range(2):
                            start = pl.multiple_of(base + (step * 2 + state) * row_block, BAND)
                            scaled_ref[pl.ds(start, BAND), column : column + targets] = block[
                                :, state * targets : (state + 1) * targets
                            ]
            return carry

        lax.fori_loop(0, span // pair, states, 0)
        for place in range(count):
            columns = slice(place * pair, (place + 1) * pair)
            value = sum(
                jnp.dot(
                    dense_ref[block, :, part * deep : (part + 1) * deep],
                    scaled_ref[block * deep : (block + 1) * deep, columns],
                    preferred_element_type=jnp.float32,
                )
                for block in range(blocks)
            )
            for time in range(2):
                piece = value[:, time * targets : (time + 1) * targets].reshape(owners, inner, targets)
                if has_total:
                    piece = piece + total_ref[place, :, time, :, :]
                out_ref[place, :, time, :, :] = piece.astype(out_ref.dtype)


def contract(jobs, part, timed, gains, dense, slabs, totals, owners, dtypes):
    slab, span = slabs[0].shape
    rows = timed.shape[2] // 2
    states = dense.shape[0] * dense.shape[2] // rows
    targets = gains.shape[2] // states
    depth = span // targets * rows
    operands = [timed, gains, dense, *slabs, *totals]
    wide = max(count for _, _, count in jobs)
    work = sum(count for _, _, count in jobs)
    return pl.pallas_call(
        functools.partial(contract_kernel, jobs, part, bool(totals)),
        out_shape=[
            jax.ShapeDtypeStruct((count, owners, 2, dense.shape[1] // owners, targets), dtype)
            for (_, _, count), dtype in zip(jobs, dtypes)
        ],
        in_specs=[WHOLE] * len(operands),
        out_specs=[WHOLE] * len(jobs),
        scratch_shapes=[
            pltpu.VMEM((4 * slab, span), jnp.bfloat16),
            pltpu.VMEM((depth, wide * 2 * targets), jnp.bfloat16),
        ],
        compiler_params=params(),
        cost_estimate=pl.CostEstimate(
            flops=4 * work * (rows * 4 * slab * span + dense.shape[1] * depth * targets),
            bytes_accessed=2 * 1024 * 1024 * work,
            transcendentals=0,
        ),
    )(*operands)


def shards(
    screened, grid_weights, greens, three_state, three_orbital, block_ids, block_counts, owners
):
    freq_count = lax.axis_size("freq")
    aux_count = lax.axis_size("aux")
    freq = lax.axis_index("freq")
    chip, core = freq // 2, freq % 2
    local_times, rows, width = screened.shape
    total_times = local_times * freq_count
    states = three_state.shape[1]
    targets = three_state.shape[2]
    block_count, slot_count = block_ids.shape
    orbitals = three_orbital.shape[2]
    block_width = orbitals // slot_count
    row_block = rows // block_count
    chips = freq_count // 2
    height = aux_count // DEPTH

    along = []
    for f in range(freq_count):
        for y in range(height):
            for z in range(DEPTH):
                far = (z + SHIFTS[z % 2][f]) % DEPTH
                along.append((f * aux_count + y * DEPTH + far, f * aux_count + y * DEPTH + z))
    across = [
        [(((y + i) % height) * DEPTH + z, y * DEPTH + z) for y in range(height) for z in range(DEPTH)]
        for i in range(height)
    ]
    flat_state = three_state.reshape(rows, states * targets)
    flat_state, screened = lax.optimization_barrier((flat_state, screened))
    span = states * targets // 2
    slabs = []
    for part in range(2):
        own = lax.ppermute(flat_state[:, part * span : (part + 1) * span], ("freq", "aux"), along)
        slabs.append([own] + [lax.ppermute(own, "aux", across[i]) for i in range(1, height)])

    place = lax.axis_index("aux").astype(jnp.int32).reshape(1)
    pieces = pick(place, screened, freq_count)
    pieces = lax.all_to_all(pieces, "freq", split_axis=0, concat_axis=0, tiled=True)

    half = jnp.arange(2, dtype=jnp.int32)[:, None, None]
    other = jnp.arange(chips, dtype=jnp.int32)[None, :, None]
    step = jnp.arange(local_times, dtype=jnp.int32)[None, None, :]
    time = ((chip + other) % chips) * 2 * local_times + ((core + 1 + half) % 2) * local_times + step
    time = time.reshape(2, chips * local_times)
    freqs = jnp.arange(total_times, dtype=jnp.int32)
    lanes = jnp.arange(total_times * BAND, dtype=jnp.int32) // BAND
    weights = jnp.repeat(grid_weights, BAND)
    table = weights * jnp.cos(
        jnp.pi * (time[:, :, None].astype(jnp.float32) + 0.5) * lanes.astype(jnp.float32) / total_times
    )
    gains = jnp.sum(jnp.where(time[:, :, None, None] == freqs[:, None], greens, 0.0), axis=2)
    gains = jnp.repeat(gains, targets, axis=2)

    device = jnp.arange(aux_count, dtype=jnp.int32)
    owned = jnp.sum(jnp.where(owners[None, :] == device[:, None], device[None, :], 0), axis=1)
    inner = orbitals // aux_count
    wanted = (owned[:, None] * inner + jnp.arange(inner, dtype=jnp.int32)[None, :]).reshape(orbitals)
    slot = jnp.arange(slot_count, dtype=jnp.int32)
    listed = block_ids[:, :, None] * block_width + jnp.arange(block_width, dtype=jnp.int32)
    listed = jnp.where(slot[None, :, None] < block_counts[:, None, None], listed, -1).reshape(block_count, orbitals)
    choose = (wanted[None, :, None] == listed[:, None, :]).astype(jnp.bfloat16)
    _, three_orbital = lax.optimization_barrier((slabs[0][0], three_orbital))
    values = three_orbital.reshape(block_count, row_block, states, orbitals)
    values = values.transpose(0, 2, 1, 3).reshape(block_count, states * row_block, orbitals)
    dense = jnp.einsum("bns,brs->bnr", choose, values, preferred_element_type=jnp.float32).astype(jnp.bfloat16)

    slabs[0][1], pieces = lax.optimization_barrier((slabs[0][1], pieces))
    timed = transform(pieces, table)
    run = functools.partial(contract, timed=timed, gains=gains, dense=dense, owners=aux_count)
    swap = [(f, f ^ 1) for f in range(freq_count)]
    jobs = ((0, 0, chips), (1, 1, chips - 1), (1, 0, 1))
    totals = list(run(jobs, 0, slabs=slabs[0], totals=[], dtypes=(jnp.float32,) * 3))
    (given,) = run(jobs[:1], 1, slabs=slabs[1], totals=totals[:1], dtypes=(jnp.bfloat16,))
    taken = lax.ppermute(given, "freq", swap)
    (kept,) = run(jobs[1:2], 1, slabs=slabs[1], totals=totals[1:2], dtypes=(jnp.float32,))
    sent = [
        (kept[i - 1] + taken[i].astype(jnp.float32)).astype(jnp.bfloat16) for i in range(1, chips)
    ]

    def chip_shift(by):
        return [(2 * x + c, 2 * ((x + by) % chips) + c) for x in range(chips) for c in range(2)]

    totals[2], sent[0] = lax.optimization_barrier((totals[2], sent[0]))
    arrived = [lax.ppermute(sent[i], "freq", chip_shift(i + 1)) for i in range(chips - 1)]
    (kept,) = run(jobs[2:], 1, slabs=slabs[1], totals=totals[2:], dtypes=(jnp.float32,))
    summed = kept[0] + taken[0].astype(jnp.float32)
    for piece in arrived:
        summed = summed + piece.astype(jnp.float32)
    spread = lax.all_to_all(summed.astype(jnp.bfloat16), "aux", split_axis=0, concat_axis=0, tiled=True)
    return jnp.sum(spread.astype(jnp.float32), axis=0)


def solution(mesh):
    return jax.shard_map(
        shards,
        mesh=mesh,
        in_specs=(
            P("freq", "aux", None),
            P(),
            P(),
            P("aux", None, None),
            P("aux", None, None),
            P("aux", None),
            P("aux"),
            P(),
        ),
        out_specs=P("freq", "aux", None),
        check_vma=False,
    )
```

```python
import functools

import jax
import jax.numpy as jnp
from jax import lax
from jax.experimental import pallas as pl
from jax.experimental.pallas import tpu as pltpu
from jax.sharding import PartitionSpec as P

BAND = 16
DEPTH = 8
SHIFTS = ((0, 4, 3, 5, 2, 6, 1, 7), (0, 4, 1, 7, 2, 6, 3, 5))
WHOLE = pl.BlockSpec(memory_space=pltpu.VMEM)


def params():
    return pltpu.CompilerParams(vmem_limit_bytes=32 * 1024 * 1024)


def pick_kernel(place_ref, screened_ref, out_ref):
    place = place_ref[0]
    row, column = place // DEPTH, place % DEPTH
    odd = column % 2
    slab = out_ref.shape[3] // 4
    for f in range(out_ref.shape[0]):
        far = lax.rem(column + jnp.where(odd == 1, SHIFTS[1][f], SHIFTS[0][f]), DEPTH)
        for i in range(4):
            start = (lax.rem(row + i, 4) * DEPTH + far) * slab
            out_ref[f, :, :, i * slab : (i + 1) * slab] = screened_ref[:, :, pl.ds(pl.multiple_of(start, slab), slab)]


def pick(place, screened, freqs):
    local, rows, width = screened.shape
    tall = rows // 4
    return pl.pallas_call(
        pick_kernel,
        out_shape=jax.ShapeDtypeStruct((freqs, local, rows, width // freqs), screened.dtype),
        grid_spec=pltpu.PrefetchScalarGridSpec(
            num_scalar_prefetch=1,
            grid=(rows // tall,),
            in_specs=[pl.BlockSpec((local, tall, width), lambda i, place: (0, i, 0))],
            out_specs=pl.BlockSpec((freqs, local, tall, width // freqs), lambda i, place: (0, 0, i, 0)),
        ),
        compiler_params=params(),
    )(place, screened)


def spread_kernel(table_ref, out_ref):
    times, wide = table_ref.shape[1:]
    lane = lax.broadcasted_iota(jnp.int32, (BAND, wide), 1) % BAND
    keep = lane == lax.broadcasted_iota(jnp.int32, (BAND, wide), 0)
    tall = times * BAND
    for half in range(2):
        for time in range(times):
            value = jnp.where(keep, table_ref[half, time : time + 1, :], 0.0)
            upper = value.astype(jnp.bfloat16)
            lower = (value - upper.astype(jnp.float32)).astype(jnp.bfloat16)
            out_ref[half, time * BAND : (time + 1) * BAND, :] = upper
            out_ref[half, tall + time * BAND : tall + (time + 1) * BAND, :] = lower


def spread_table(table):
    _, times, wide = table.shape
    return pl.pallas_call(
        spread_kernel,
        out_shape=jax.ShapeDtypeStruct((2, 2 * times * BAND, wide), jnp.bfloat16),
        in_specs=[WHOLE],
        out_specs=WHOLE,
        compiler_params=params(),
    )(table)


def mix_kernel(pieces_ref, mix_ref, out_ref):
    sources, local, rows, width = pieces_ref.shape
    freqs = sources * local
    places = out_ref.shape[1]
    pair = 2 * BAND
    tall = places * pair
    for band in range(rows // BAND):
        piece = pieces_ref[:, :, band * BAND : (band + 1) * BAND, :].reshape(freqs * BAND, width)
        for half in range(2):
            mixed = jnp.dot(mix_ref[half], piece, preferred_element_type=jnp.float32)
            mixed = (mixed[:tall] + mixed[tall:]).astype(jnp.bfloat16)
            for place in range(places):
                out_ref[half, place, band * pair : (band + 1) * pair, :] = mixed[place * pair : (place + 1) * pair]


def transform(pieces, mix):
    sources, local, rows, width = pieces.shape
    times = mix.shape[1] // (2 * BAND)
    return pl.pallas_call(
        mix_kernel,
        out_shape=jax.ShapeDtypeStruct((2, times // 2, 2 * rows, width), jnp.bfloat16),
        in_specs=[WHOLE] * 2,
        out_specs=WHOLE,
        compiler_params=params(),
    )(pieces, mix)


def contract_kernel(jobs, part, has_total, *refs):
    timed_ref, gains_ref, dense_ref = refs[:3]
    slabs = refs[3:7]
    refs = refs[7:]
    totals = [None] * len(jobs)
    if has_total:
        totals, refs = refs[: len(jobs)], refs[len(jobs) :]
    outs, (state_ref, scaled_ref) = refs[: len(jobs)], refs[len(jobs) :]
    slab = slabs[0].shape[0]
    for i in range(4):
        state_ref[i * slab : (i + 1) * slab, :] = slabs[i][...]
    span = state_ref.shape[1]
    blocks = dense_ref.shape[0]
    deep = scaled_ref.shape[0] // blocks
    tall, depth = timed_ref.shape[2:]
    bands = tall // (2 * BAND)
    bands_in = bands // blocks
    row_block = bands_in * BAND
    owners, inner, targets = outs[0].shape[1], outs[0].shape[3], outs[0].shape[4]
    pair = 2 * targets

    for (half, first, count), total_ref, out_ref in zip(jobs, totals, outs):
        timed = timed_ref[half, first : first + count].reshape(count * tall, depth)

        def states(step, carry):
            columns = pl.ds(pl.multiple_of(step * pair, pair), pair)
            contracted = jnp.dot(timed, state_ref[:, columns], preferred_element_type=jnp.float32)
            gains = gains_ref[half, :, pl.ds(pl.multiple_of(part * span + step * pair, pair), pair)]
            for place in range(count):
                for time in range(2):
                    at = 2 * (first + place) + time
                    gain = gains[at : at + 1, :]
                    column = (2 * place + time) * targets
                    for band in range(bands):
                        row = place * tall + (2 * band + time) * BAND
                        block = (contracted[row : row + BAND, :] * gain).astype(jnp.bfloat16)
                        base = (band // bands_in) * deep + (band % bands_in) * BAND
                        for state in range(2):
                            start = pl.multiple_of(base + (step * 2 + state) * row_block, BAND)
                            scaled_ref[pl.ds(start, BAND), column : column + targets] = block[
                                :, state * targets : (state + 1) * targets
                            ]
            return carry

        lax.fori_loop(0, span // pair, states, 0)
        for place in range(count):
            columns = slice(place * pair, (place + 1) * pair)
            value = sum(
                jnp.dot(
                    dense_ref[block, :, part * deep : (part + 1) * deep],
                    scaled_ref[block * deep : (block + 1) * deep, columns],
                    preferred_element_type=jnp.float32,
                )
                for block in range(blocks)
            )
            for time in range(2):
                piece = value[:, time * targets : (time + 1) * targets].reshape(owners, inner, targets)
                if has_total:
                    piece = piece + total_ref[place, :, time, :, :]
                out_ref[place, :, time, :, :] = piece.astype(out_ref.dtype)


def contract(jobs, part, timed, gains, dense, slabs, totals, owners, dtypes):
    slab, span = slabs[0].shape
    rows = timed.shape[2] // 2
    states = dense.shape[0] * dense.shape[2] // rows
    targets = gains.shape[2] // states
    depth = span // targets * rows
    operands = [timed, gains, dense, *slabs, *totals]
    wide = max(count for _, _, count in jobs)
    work = sum(count for _, _, count in jobs)
    return pl.pallas_call(
        functools.partial(contract_kernel, jobs, part, bool(totals)),
        out_shape=[
            jax.ShapeDtypeStruct((count, owners, 2, dense.shape[1] // owners, targets), dtype)
            for (_, _, count), dtype in zip(jobs, dtypes)
        ],
        in_specs=[WHOLE] * len(operands),
        out_specs=[WHOLE] * len(jobs),
        scratch_shapes=[
            pltpu.VMEM((4 * slab, span), jnp.bfloat16),
            pltpu.VMEM((depth, wide * 2 * targets), jnp.bfloat16),
        ],
        compiler_params=params(),
        cost_estimate=pl.CostEstimate(
            flops=4 * work * (rows * 4 * slab * span + dense.shape[1] * depth * targets),
            bytes_accessed=2 * 1024 * 1024 * work,
            transcendentals=0,
        ),
    )(*operands)


def shards(
    screened, grid_weights, greens, three_state, three_orbital, block_ids, block_counts, owners
):
    freq_count = lax.axis_size("freq")
    aux_count = lax.axis_size("aux")
    freq = lax.axis_index("freq")
    chip, core = freq // 2, freq % 2
    local_times, rows, width = screened.shape
    total_times = local_times * freq_count
    states = three_state.shape[1]
    targets = three_state.shape[2]
    block_count, slot_count = block_ids.shape
    orbitals = three_orbital.shape[2]
    block_width = orbitals // slot_count
    row_block = rows // block_count
    chips = freq_count // 2
    height = aux_count // DEPTH

    along = []
    for f in range(freq_count):
        for y in range(height):
            for z in range(DEPTH):
                far = (z + SHIFTS[z % 2][f]) % DEPTH
                along.append((f * aux_count + y * DEPTH + far, f * aux_count + y * DEPTH + z))
    across = [
        [(((y + i) % height) * DEPTH + z, y * DEPTH + z) for y in range(height) for z in range(DEPTH)]
        for i in range(height)
    ]
    flat_state = three_state.reshape(rows, states * targets)
    flat_state, screened = lax.optimization_barrier((flat_state, screened))
    span = states * targets // 2
    parts = [flat_state[:, part * span : (part + 1) * span] for part in range(2)]
    own = lax.ppermute(parts[0], ("freq", "aux"), along)
    slabs = [[own] + [lax.ppermute(own, "aux", across[i]) for i in range(1, height)]]
    parts[1], slabs[0][0] = lax.optimization_barrier((parts[1], slabs[0][0]))
    own = lax.ppermute(parts[1], ("freq", "aux"), along)
    slabs.append([own])
    for i in range(1, height):
        ready, slabs[0][i] = lax.optimization_barrier((own, slabs[0][i]))
        slabs[1].append(lax.ppermute(ready, "aux", across[i]))

    place = lax.axis_index("aux").astype(jnp.int32).reshape(1)
    pieces = pick(place, screened, freq_count)
    pieces = lax.all_to_all(pieces, "freq", split_axis=0, concat_axis=0, tiled=True)

    half = jnp.arange(2, dtype=jnp.int32)[:, None, None]
    other = jnp.arange(chips, dtype=jnp.int32)[None, :, None]
    step = jnp.arange(local_times, dtype=jnp.int32)[None, None, :]
    time = ((chip + other) % chips) * 2 * local_times + ((core + 1 + half) % 2) * local_times + step
    time = time.reshape(2, chips * local_times)
    freqs = jnp.arange(total_times, dtype=jnp.int32)
    lanes = jnp.arange(total_times * BAND, dtype=jnp.int32) // BAND
    weights = jnp.repeat(grid_weights, BAND)
    table = weights * jnp.cos(
        jnp.pi * (time[:, :, None].astype(jnp.float32) + 0.5) * lanes.astype(jnp.float32) / total_times
    )
    gains = jnp.sum(jnp.where(time[:, :, None, None] == freqs[:, None], greens, 0.0), axis=2)
    gains = jnp.repeat(gains, targets, axis=2)

    device = jnp.arange(aux_count, dtype=jnp.int32)
    owned = jnp.sum(jnp.where(owners[None, :] == device[:, None], device[None, :], 0), axis=1)
    inner = orbitals // aux_count
    wanted = (owned[:, None] * inner + jnp.arange(inner, dtype=jnp.int32)[None, :]).reshape(orbitals)
    slot = jnp.arange(slot_count, dtype=jnp.int32)
    listed = block_ids[:, :, None] * block_width + jnp.arange(block_width, dtype=jnp.int32)
    listed = jnp.where(slot[None, :, None] < block_counts[:, None, None], listed, -1).reshape(block_count, orbitals)
    choose = (wanted[None, :, None] == listed[:, None, :]).astype(jnp.bfloat16)
    _, three_orbital = lax.optimization_barrier((slabs[0][0], three_orbital))
    values = three_orbital.reshape(block_count, row_block, states, orbitals)
    values = values.transpose(0, 2, 1, 3).reshape(block_count, states * row_block, orbitals)
    dense = jnp.einsum("bns,brs->bnr", choose, values, preferred_element_type=jnp.float32).astype(jnp.bfloat16)

    slabs[0][1], pieces = lax.optimization_barrier((slabs[0][1], pieces))
    timed = transform(pieces, spread_table(table))
    run = functools.partial(contract, timed=timed, gains=gains, dense=dense, owners=aux_count)
    swap = [(f, f ^ 1) for f in range(freq_count)]
    jobs = ((0, 0, chips), (1, 1, chips - 1), (1, 0, 1))
    totals = list(run(jobs, 0, slabs=slabs[0], totals=[], dtypes=(jnp.float32,) * 3))
    (given,) = run(jobs[:1], 1, slabs=slabs[1], totals=totals[:1], dtypes=(jnp.bfloat16,))
    taken = lax.ppermute(given, "freq", swap)
    (kept,) = run(jobs[1:2], 1, slabs=slabs[1], totals=totals[1:2], dtypes=(jnp.float32,))
    sent = [
        (kept[i - 1] + taken[i].astype(jnp.float32)).astype(jnp.bfloat16) for i in range(1, chips)
    ]

    def chip_shift(by):
        return [(2 * x + c, 2 * ((x + by) % chips) + c) for x in range(chips) for c in range(2)]

    totals[2], sent[0] = lax.optimization_barrier((totals[2], sent[0]))
    arrived = [lax.ppermute(sent[i], "freq", chip_shift(i + 1)) for i in range(chips - 1)]
    (kept,) = run(jobs[2:], 1, slabs=slabs[1], totals=totals[2:], dtypes=(jnp.float32,))
    summed = kept[0] + taken[0].astype(jnp.float32)
    for piece in arrived:
        summed = summed + piece.astype(jnp.float32)
    spread = lax.all_to_all(summed.astype(jnp.bfloat16), "aux", split_axis=0, concat_axis=0, tiled=True)
    return jnp.sum(spread.astype(jnp.float32), axis=0)


def solution(mesh):
    return jax.shard_map(
        shards,
        mesh=mesh,
        in_specs=(
            P("freq", "aux", None),
            P(),
            P(),
            P("aux", None, None),
            P("aux", None, None),
            P("aux", None),
            P("aux"),
            P(),
        ),
        out_specs=P("freq", "aux", None),
        check_vma=False,
    )
```

```python
import functools

import jax
import jax.numpy as jnp
from jax import lax
from jax.experimental import pallas as pl
from jax.experimental.pallas import tpu as pltpu
from jax.sharding import PartitionSpec as P

BAND = 16
DEPTH = 8
SHIFTS = ((0, 4, 3, 5, 2, 6, 1, 7), (0, 4, 1, 7, 2, 6, 3, 5))
WHOLE = pl.BlockSpec(memory_space=pltpu.VMEM)


def params(mebibytes=32):
    return pltpu.CompilerParams(vmem_limit_bytes=mebibytes * 1024 * 1024)


def pick_kernel(place_ref, screened_ref, out_ref):
    place = place_ref[0]
    row, column = place // DEPTH, place % DEPTH
    odd = column % 2
    slab = out_ref.shape[3] // 4
    for f in range(out_ref.shape[0]):
        far = lax.rem(column + jnp.where(odd == 1, SHIFTS[1][f], SHIFTS[0][f]), DEPTH)
        for i in range(4):
            start = (lax.rem(row + i, 4) * DEPTH + far) * slab
            out_ref[f, :, :, i * slab : (i + 1) * slab] = screened_ref[:, :, pl.ds(pl.multiple_of(start, slab), slab)]


def pick(place, screened, freqs):
    local, rows, width = screened.shape
    tall = rows // 4
    return pl.pallas_call(
        pick_kernel,
        out_shape=jax.ShapeDtypeStruct((freqs, local, rows, width // freqs), screened.dtype),
        grid_spec=pltpu.PrefetchScalarGridSpec(
            num_scalar_prefetch=1,
            grid=(rows // tall,),
            in_specs=[pl.BlockSpec((local, tall, width), lambda i, place: (0, i, 0))],
            out_specs=pl.BlockSpec((freqs, local, tall, width // freqs), lambda i, place: (0, 0, i, 0)),
        ),
        compiler_params=params(60),
    )(place, screened)


def spread_kernel(table_ref, out_ref):
    times, wide = table_ref.shape[1:]
    lane = lax.broadcasted_iota(jnp.int32, (BAND, wide), 1) % BAND
    keep = lane == lax.broadcasted_iota(jnp.int32, (BAND, wide), 0)
    tall = times * BAND
    for half in range(2):
        for time in range(times):
            value = jnp.where(keep, table_ref[half, time : time + 1, :], 0.0)
            upper = value.astype(jnp.bfloat16)
            lower = (value - upper.astype(jnp.float32)).astype(jnp.bfloat16)
            out_ref[half, time * BAND : (time + 1) * BAND, :] = upper
            out_ref[half, tall + time * BAND : tall + (time + 1) * BAND, :] = lower


def spread_table(table):
    _, times, wide = table.shape
    return pl.pallas_call(
        spread_kernel,
        out_shape=jax.ShapeDtypeStruct((2, 2 * times * BAND, wide), jnp.bfloat16),
        in_specs=[WHOLE],
        out_specs=WHOLE,
        compiler_params=params(),
    )(table)


def mix_kernel(pieces_ref, mix_ref, out_ref):
    sources, local, rows, width = pieces_ref.shape
    freqs = sources * local
    places = out_ref.shape[1]
    pair = 2 * BAND
    tall = places * pair
    mix = mix_ref[...].reshape(4 * tall, freqs * BAND)
    for band in range(rows // BAND):
        piece = pieces_ref[:, :, band * BAND : (band + 1) * BAND, :].reshape(freqs * BAND, width)
        both = jnp.dot(mix, piece, preferred_element_type=jnp.float32)
        for half in range(2):
            upper = both[2 * half * tall : (2 * half + 1) * tall]
            lower = both[(2 * half + 1) * tall : (2 * half + 2) * tall]
            mixed = (upper + lower).astype(jnp.bfloat16)
            for place in range(places):
                out_ref[half, place, band * pair : (band + 1) * pair, :] = mixed[place * pair : (place + 1) * pair]


def transform(pieces, mix):
    sources, local, rows, width = pieces.shape
    times = mix.shape[1] // (2 * BAND)
    return pl.pallas_call(
        mix_kernel,
        out_shape=jax.ShapeDtypeStruct((2, times // 2, 2 * rows, width), jnp.bfloat16),
        in_specs=[WHOLE] * 2,
        out_specs=WHOLE,
        compiler_params=params(),
    )(pieces, mix)


def contract_kernel(jobs, part, has_total, *refs):
    timed_ref, gains_ref, dense_ref = refs[:3]
    slabs = refs[3:7]
    refs = refs[7:]
    totals = [None] * len(jobs)
    if has_total:
        totals, refs = refs[: len(jobs)], refs[len(jobs) :]
    outs, (state_ref, scaled_ref) = refs[: len(jobs)], refs[len(jobs) :]
    slab = slabs[0].shape[0]
    for i in range(4):
        state_ref[i * slab : (i + 1) * slab, :] = slabs[i][...]
    span = state_ref.shape[1]
    blocks = dense_ref.shape[0]
    deep = scaled_ref.shape[0] // blocks
    tall, depth = timed_ref.shape[2:]
    bands = tall // (2 * BAND)
    bands_in = bands // blocks
    row_block = bands_in * BAND
    owners, inner, targets = outs[0].shape[1], outs[0].shape[3], outs[0].shape[4]
    pair = 2 * targets

    for (half, first, count), total_ref, out_ref in zip(jobs, totals, outs):
        timed = timed_ref[half, first : first + count].reshape(count * tall, depth)

        def states(step, carry):
            columns = pl.ds(pl.multiple_of(step * pair, pair), pair)
            contracted = jnp.dot(timed, state_ref[:, columns], preferred_element_type=jnp.float32)
            gains = gains_ref[half, :, pl.ds(pl.multiple_of(part * span + step * pair, pair), pair)]
            for place in range(count):
                for time in range(2):
                    at = 2 * (first + place) + time
                    gain = gains[at : at + 1, :]
                    column = (2 * place + time) * targets
                    for band in range(bands):
                        row = place * tall + (2 * band + time) * BAND
                        block = (contracted[row : row + BAND, :] * gain).astype(jnp.bfloat16)
                        base = (band // bands_in) * deep + (band % bands_in) * BAND
                        for state in range(2):
                            start = pl.multiple_of(base + (step * 2 + state) * row_block, BAND)
                            scaled_ref[pl.ds(start, BAND), column : column + targets] = block[
                                :, state * targets : (state + 1) * targets
                            ]
            return carry

        lax.fori_loop(0, span // pair, states, 0)
        for place in range(count):
            columns = slice(place * pair, (place + 1) * pair)
            value = sum(
                jnp.dot(
                    dense_ref[block, :, part * deep : (part + 1) * deep],
                    scaled_ref[block * deep : (block + 1) * deep, columns],
                    preferred_element_type=jnp.float32,
                )
                for block in range(blocks)
            )
            for time in range(2):
                piece = value[:, time * targets : (time + 1) * targets].reshape(owners, inner, targets)
                if has_total:
                    piece = piece + total_ref[place, :, time, :, :]
                out_ref[place, :, time, :, :] = piece.astype(out_ref.dtype)


def contract(jobs, part, timed, gains, dense, slabs, totals, owners, dtypes):
    slab, span = slabs[0].shape
    rows = timed.shape[2] // 2
    states = dense.shape[0] * dense.shape[2] // rows
    targets = gains.shape[2] // states
    depth = span // targets * rows
    operands = [timed, gains, dense, *slabs, *totals]
    wide = max(count for _, _, count in jobs)
    work = sum(count for _, _, count in jobs)
    return pl.pallas_call(
        functools.partial(contract_kernel, jobs, part, bool(totals)),
        out_shape=[
            jax.ShapeDtypeStruct((count, owners, 2, dense.shape[1] // owners, targets), dtype)
            for (_, _, count), dtype in zip(jobs, dtypes)
        ],
        in_specs=[WHOLE] * len(operands),
        out_specs=[WHOLE] * len(jobs),
        scratch_shapes=[
            pltpu.VMEM((4 * slab, span), jnp.bfloat16),
            pltpu.VMEM((depth, wide * 2 * targets), jnp.bfloat16),
        ],
        compiler_params=params(),
        cost_estimate=pl.CostEstimate(
            flops=4 * work * (rows * 4 * slab * span + dense.shape[1] * depth * targets),
            bytes_accessed=2 * 1024 * 1024 * work,
            transcendentals=0,
        ),
    )(*operands)


def shards(
    screened, grid_weights, greens, three_state, three_orbital, block_ids, block_counts, owners
):
    freq_count = lax.axis_size("freq")
    aux_count = lax.axis_size("aux")
    freq = lax.axis_index("freq")
    chip, core = freq // 2, freq % 2
    local_times, rows, width = screened.shape
    total_times = local_times * freq_count
    states = three_state.shape[1]
    targets = three_state.shape[2]
    block_count, slot_count = block_ids.shape
    orbitals = three_orbital.shape[2]
    block_width = orbitals // slot_count
    row_block = rows // block_count
    chips = freq_count // 2
    height = aux_count // DEPTH

    along = []
    for f in range(freq_count):
        for y in range(height):
            for z in range(DEPTH):
                far = (z + SHIFTS[z % 2][f]) % DEPTH
                along.append((f * aux_count + y * DEPTH + far, f * aux_count + y * DEPTH + z))
    across = [
        [(((y + i) % height) * DEPTH + z, y * DEPTH + z) for y in range(height) for z in range(DEPTH)]
        for i in range(height)
    ]
    place = lax.axis_index("aux").astype(jnp.int32).reshape(1)
    pieces = pick(place, screened, freq_count)
    pieces, three_state = lax.optimization_barrier((pieces, three_state))
    pieces = lax.all_to_all(pieces, "freq", split_axis=0, concat_axis=0, tiled=True)

    def after(value, done):
        return lax.optimization_barrier((value, done))

    flat_state = three_state.reshape(rows, states * targets)
    span = states * targets // 2
    first, second = (flat_state[:, part * span : (part + 1) * span] for part in range(2))
    own = lax.ppermute(first, ("freq", "aux"), along)
    far = lax.ppermute(second, "aux", across[2])
    slabs = [[own] + [lax.ppermute(own, "aux", across[i]) for i in range(1, height)]]
    second, slabs[0][0] = after(second, slabs[0][0])
    own = lax.ppermute(second, ("freq", "aux"), along)
    far = lax.ppermute(far, ("freq", "aux"), along)
    slabs.append([own, own, far, own])
    for i in (1, 3):
        ready, slabs[0][i] = after(own, slabs[0][i])
        slabs[1][i] = lax.ppermute(ready, "aux", across[i])

    half = jnp.arange(2, dtype=jnp.int32)[:, None, None]
    other = jnp.arange(chips, dtype=jnp.int32)[None, :, None]
    step = jnp.arange(local_times, dtype=jnp.int32)[None, None, :]
    time = ((chip + other) % chips) * 2 * local_times + ((core + 1 + half) % 2) * local_times + step
    time = time.reshape(2, chips * local_times)
    freqs = jnp.arange(total_times, dtype=jnp.int32)
    lanes = jnp.arange(total_times * BAND, dtype=jnp.int32) // BAND
    weights = jnp.repeat(grid_weights, BAND)
    table = weights * jnp.cos(
        jnp.pi * (time[:, :, None].astype(jnp.float32) + 0.5) * lanes.astype(jnp.float32) / total_times
    )
    gains = jnp.sum(jnp.where(time[:, :, None, None] == freqs[:, None], greens, 0.0), axis=2)
    gains = jnp.repeat(gains, targets, axis=2)

    device = jnp.arange(aux_count, dtype=jnp.int32)
    owned = jnp.sum(jnp.where(owners[None, :] == device[:, None], device[None, :], 0), axis=1)
    inner = orbitals // aux_count
    wanted = (owned[:, None] * inner + jnp.arange(inner, dtype=jnp.int32)[None, :]).reshape(orbitals)
    slot = jnp.arange(slot_count, dtype=jnp.int32)
    listed = block_ids[:, :, None] * block_width + jnp.arange(block_width, dtype=jnp.int32)
    listed = jnp.where(slot[None, :, None] < block_counts[:, None, None], listed, -1).reshape(block_count, orbitals)
    choose = (wanted[None, :, None] == listed[:, None, :]).astype(jnp.bfloat16)
    _, three_orbital = lax.optimization_barrier((slabs[0][0], three_orbital))
    values = three_orbital.reshape(block_count, row_block, states, orbitals)
    values = values.transpose(0, 2, 1, 3).reshape(block_count, states * row_block, orbitals)
    dense = jnp.einsum("bns,brs->bnr", choose, values, preferred_element_type=jnp.float32).astype(jnp.bfloat16)

    slabs[0][1], pieces = lax.optimization_barrier((slabs[0][1], pieces))
    timed = transform(pieces, spread_table(table))
    run = functools.partial(contract, timed=timed, gains=gains, dense=dense, owners=aux_count)
    swap = [(f, f ^ 1) for f in range(freq_count)]
    jobs = ((0, 0, chips), (1, 1, chips - 1), (1, 0, 1))
    totals = list(run(jobs, 0, slabs=slabs[0], totals=[], dtypes=(jnp.float32,) * 3))
    (given,) = run(jobs[:1], 1, slabs=slabs[1], totals=totals[:1], dtypes=(jnp.bfloat16,))
    taken = lax.ppermute(given, "freq", swap)
    (kept,) = run(jobs[1:2], 1, slabs=slabs[1], totals=totals[1:2], dtypes=(jnp.float32,))
    sent = [
        (kept[i - 1] + taken[i].astype(jnp.float32)).astype(jnp.bfloat16) for i in range(1, chips)
    ]

    def chip_shift(by):
        return [(2 * x + c, 2 * ((x + by) % chips) + c) for x in range(chips) for c in range(2)]

    totals[2], sent[0] = lax.optimization_barrier((totals[2], sent[0]))
    arrived = [lax.ppermute(sent[i], "freq", chip_shift(i + 1)) for i in range(chips - 1)]
    (kept,) = run(jobs[2:], 1, slabs=slabs[1], totals=totals[2:], dtypes=(jnp.float32,))
    summed = kept[0] + taken[0].astype(jnp.float32)
    for piece in arrived:
        summed = summed + piece.astype(jnp.float32)
    spread = lax.all_to_all(summed.astype(jnp.bfloat16), "aux", split_axis=0, concat_axis=0, tiled=True)
    return jnp.sum(spread.astype(jnp.float32), axis=0)


def solution(mesh):
    return jax.shard_map(
        shards,
        mesh=mesh,
        in_specs=(
            P("freq", "aux", None),
            P(),
            P(),
            P("aux", None, None),
            P("aux", None, None),
            P("aux", None),
            P("aux"),
            P(),
        ),
        out_specs=P("freq", "aux", None),
        check_vma=False,
    )
```

```python
import functools

import jax
import jax.numpy as jnp
from jax import lax
from jax.experimental import pallas as pl
from jax.experimental.pallas import tpu as pltpu
from jax.sharding import PartitionSpec as P

BAND = 16
DEPTH = 8
SHIFTS = ((0, 4, 3, 5, 2, 6, 1, 7), (0, 4, 1, 7, 2, 6, 3, 5))
WHOLE = pl.BlockSpec(memory_space=pltpu.VMEM)


def params(mebibytes=24):
    return pltpu.CompilerParams(vmem_limit_bytes=mebibytes * 1024 * 1024)


def pick_kernel(place_ref, screened_ref, out_ref, piece_ref, sems):
    place = place_ref[0]
    row, column = place // DEPTH, place % DEPTH
    odd = column % 2
    slab = out_ref.shape[3] // 4
    copies = []
    for f in range(out_ref.shape[0]):
        far = lax.rem(column + jnp.where(odd == 1, SHIFTS[1][f], SHIFTS[0][f]), DEPTH)
        for i in range(4):
            start = (lax.rem(row + i, 4) * DEPTH + far) * slab
            piece_ref[f, :, :, i * slab : (i + 1) * slab] = screened_ref[:, :, pl.ds(pl.multiple_of(start, slab), slab)]
        copies.append(pltpu.make_async_copy(piece_ref.at[f], out_ref.at[f], sems.at[f]))
        copies[-1].start()
    for copy in copies:
        copy.wait()


def pick(place, screened, freqs):
    local, rows, width = screened.shape
    shape = (freqs, local, rows, width // freqs)
    return pl.pallas_call(
        pick_kernel,
        out_shape=jax.ShapeDtypeStruct(shape, screened.dtype),
        in_specs=[pl.BlockSpec(memory_space=pltpu.SMEM), WHOLE],
        out_specs=pl.BlockSpec(memory_space=pl.ANY),
        scratch_shapes=[pltpu.VMEM(shape, screened.dtype), pltpu.SemaphoreType.DMA((freqs,))],
        compiler_params=params(16),
    )(place, screened)


def spread_kernel(table_ref, out_ref):
    times, wide = table_ref.shape[1:]
    lane = lax.broadcasted_iota(jnp.int32, (BAND, wide), 1) % BAND
    keep = lane == lax.broadcasted_iota(jnp.int32, (BAND, wide), 0)
    tall = times * BAND
    for half in range(2):
        for time in range(times):
            value = jnp.where(keep, table_ref[half, time : time + 1, :], 0.0)
            upper = value.astype(jnp.bfloat16)
            lower = (value - upper.astype(jnp.float32)).astype(jnp.bfloat16)
            out_ref[half, time * BAND : (time + 1) * BAND, :] = upper
            out_ref[half, tall + time * BAND : tall + (time + 1) * BAND, :] = lower


def spread_table(table):
    _, times, wide = table.shape
    return pl.pallas_call(
        spread_kernel,
        out_shape=jax.ShapeDtypeStruct((2, 2 * times * BAND, wide), jnp.bfloat16),
        in_specs=[WHOLE],
        out_specs=WHOLE,
        compiler_params=params(),
    )(table)


def mix_kernel(pieces_ref, mix_ref, out_ref):
    sources, local, rows, width = pieces_ref.shape
    freqs = sources * local
    places = out_ref.shape[1]
    pair = 2 * BAND
    tall = places * pair
    mix = mix_ref[...].reshape(4 * tall, freqs * BAND)
    for band in range(rows // BAND):
        piece = pieces_ref[:, :, band * BAND : (band + 1) * BAND, :].reshape(freqs * BAND, width)
        both = jnp.dot(mix, piece, preferred_element_type=jnp.float32)
        for half in range(2):
            upper = both[2 * half * tall : (2 * half + 1) * tall]
            lower = both[(2 * half + 1) * tall : (2 * half + 2) * tall]
            mixed = (upper + lower).astype(jnp.bfloat16)
            for place in range(places):
                out_ref[half, place, band * pair : (band + 1) * pair, :] = mixed[place * pair : (place + 1) * pair]


def transform(pieces, mix):
    sources, local, rows, width = pieces.shape
    times = mix.shape[1] // (2 * BAND)
    return pl.pallas_call(
        mix_kernel,
        out_shape=jax.ShapeDtypeStruct((2, times // 2, 2 * rows, width), jnp.bfloat16),
        in_specs=[WHOLE] * 2,
        out_specs=WHOLE,
        compiler_params=params(),
    )(pieces, mix)


def contract_kernel(jobs, part, has_total, *refs):
    timed_ref, gains_ref, dense_ref = refs[:3]
    slabs = refs[3:7]
    refs = refs[7:]
    totals = [None] * len(jobs)
    if has_total:
        totals, refs = refs[: len(jobs)], refs[len(jobs) :]
    outs, (state_ref, scaled_ref) = refs[: len(jobs)], refs[len(jobs) :]
    slab = slabs[0].shape[0]
    for i in range(4):
        state_ref[i * slab : (i + 1) * slab, :] = slabs[i][...]
    span = state_ref.shape[1]
    blocks = dense_ref.shape[0]
    deep = scaled_ref.shape[0] // blocks
    tall, depth = timed_ref.shape[2:]
    bands = tall // (2 * BAND)
    bands_in = bands // blocks
    row_block = bands_in * BAND
    owners, inner, targets = outs[0].shape[1], outs[0].shape[3], outs[0].shape[4]
    pair = 2 * targets

    for (half, first, count), total_ref, out_ref in zip(jobs, totals, outs):
        timed = timed_ref[half, first : first + count].reshape(count * tall, depth)

        def states(step, carry):
            columns = pl.ds(pl.multiple_of(step * pair, pair), pair)
            contracted = jnp.dot(timed, state_ref[:, columns], preferred_element_type=jnp.float32)
            gains = gains_ref[half, :, pl.ds(pl.multiple_of(part * span + step * pair, pair), pair)]
            for place in range(count):
                for time in range(2):
                    at = 2 * (first + place) + time
                    gain = gains[at : at + 1, :]
                    column = (2 * place + time) * targets
                    for band in range(bands):
                        row = place * tall + (2 * band + time) * BAND
                        block = (contracted[row : row + BAND, :] * gain).astype(jnp.bfloat16)
                        base = (band // bands_in) * deep + (band % bands_in) * BAND
                        for state in range(2):
                            start = pl.multiple_of(base + (step * 2 + state) * row_block, BAND)
                            scaled_ref[pl.ds(start, BAND), column : column + targets] = block[
                                :, state * targets : (state + 1) * targets
                            ]
            return carry

        lax.fori_loop(0, span // pair, states, 0)
        for place in range(count):
            columns = slice(place * pair, (place + 1) * pair)
            value = sum(
                jnp.dot(
                    dense_ref[block, :, part * deep : (part + 1) * deep],
                    scaled_ref[block * deep : (block + 1) * deep, columns],
                    preferred_element_type=jnp.float32,
                )
                for block in range(blocks)
            )
            for time in range(2):
                piece = value[:, time * targets : (time + 1) * targets].reshape(owners, inner, targets)
                if has_total:
                    piece = piece + total_ref[place, :, time, :, :]
                out_ref[place, :, time, :, :] = piece.astype(out_ref.dtype)


def contract(jobs, part, timed, gains, dense, slabs, totals, owners, dtypes):
    slab, span = slabs[0].shape
    rows = timed.shape[2] // 2
    states = dense.shape[0] * dense.shape[2] // rows
    targets = gains.shape[2] // states
    depth = span // targets * rows
    operands = [timed, gains, dense, *slabs, *totals]
    wide = max(count for _, _, count in jobs)
    work = sum(count for _, _, count in jobs)
    return pl.pallas_call(
        functools.partial(contract_kernel, jobs, part, bool(totals)),
        out_shape=[
            jax.ShapeDtypeStruct((count, owners, 2, dense.shape[1] // owners, targets), dtype)
            for (_, _, count), dtype in zip(jobs, dtypes)
        ],
        in_specs=[WHOLE] * len(operands),
        out_specs=[WHOLE] * len(jobs),
        scratch_shapes=[
            pltpu.VMEM((4 * slab, span), jnp.bfloat16),
            pltpu.VMEM((depth, wide * 2 * targets), jnp.bfloat16),
        ],
        compiler_params=params(),
        cost_estimate=pl.CostEstimate(
            flops=4 * work * (rows * 4 * slab * span + dense.shape[1] * depth * targets),
            bytes_accessed=2 * 1024 * 1024 * work,
            transcendentals=0,
        ),
    )(*operands)


def shards(
    screened, grid_weights, greens, three_state, three_orbital, block_ids, block_counts, owners
):
    freq_count = lax.axis_size("freq")
    aux_count = lax.axis_size("aux")
    freq = lax.axis_index("freq")
    chip, core = freq // 2, freq % 2
    local_times, rows, width = screened.shape
    total_times = local_times * freq_count
    states = three_state.shape[1]
    targets = three_state.shape[2]
    block_count, slot_count = block_ids.shape
    orbitals = three_orbital.shape[2]
    block_width = orbitals // slot_count
    row_block = rows // block_count
    chips = freq_count // 2
    height = aux_count // DEPTH

    along = []
    for f in range(freq_count):
        for y in range(height):
            for z in range(DEPTH):
                far = (z + SHIFTS[z % 2][f]) % DEPTH
                along.append((f * aux_count + y * DEPTH + far, f * aux_count + y * DEPTH + z))
    across = [
        [(((y + i) % height) * DEPTH + z, y * DEPTH + z) for y in range(height) for z in range(DEPTH)]
        for i in range(height)
    ]
    flat_state = three_state.reshape(rows, states * targets)
    flat_state, screened = lax.optimization_barrier((flat_state, screened))
    span = states * targets // 2
    first, second = (flat_state[:, part * span : (part + 1) * span] for part in range(2))
    own = lax.ppermute(first, ("freq", "aux"), along)
    far = lax.ppermute(second, "aux", across[2])
    own, far = lax.optimization_barrier((own, far))
    slabs = [[own] + [lax.ppermute(own, "aux", across[i]) for i in range(1, height)]]
    second, far, slabs[0][1] = lax.optimization_barrier((second, far, slabs[0][1]))
    own = lax.ppermute(second, ("freq", "aux"), along)
    far = lax.ppermute(far, ("freq", "aux"), along)
    slabs.append([own, None, far, None])
    for i in (1, 3):
        ready, slabs[0][i] = lax.optimization_barrier((own, slabs[0][i]))
        slabs[1][i] = lax.ppermute(ready, "aux", across[i])

    device = jnp.arange(aux_count, dtype=jnp.int32)
    owned = jnp.sum(jnp.where(owners[None, :] == device[:, None], device[None, :], 0), axis=1)
    inner = orbitals // aux_count
    wanted = (owned[:, None] * inner + jnp.arange(inner, dtype=jnp.int32)[None, :]).reshape(orbitals)
    slot = jnp.arange(slot_count, dtype=jnp.int32)
    listed = block_ids[:, :, None] * block_width + jnp.arange(block_width, dtype=jnp.int32)
    listed = jnp.where(slot[None, :, None] < block_counts[:, None, None], listed, -1).reshape(block_count, orbitals)
    choose = (wanted[None, :, None] == listed[:, None, :]).astype(jnp.bfloat16)
    _, three_orbital = lax.optimization_barrier((slabs[0][1], three_orbital))
    values = three_orbital.reshape(block_count, row_block, states, orbitals)
    values = values.transpose(0, 2, 1, 3).reshape(block_count, states * row_block, orbitals)
    dense = jnp.einsum("bns,brs->bnr", choose, values, preferred_element_type=jnp.float32).astype(jnp.bfloat16)
    place = lax.axis_index("aux").astype(jnp.int32).reshape(1)
    pieces = pick(place, screened, freq_count)
    pieces = lax.all_to_all(pieces, "freq", split_axis=0, concat_axis=0, tiled=True)

    half = jnp.arange(2, dtype=jnp.int32)[:, None, None]
    other = jnp.arange(chips, dtype=jnp.int32)[None, :, None]
    step = jnp.arange(local_times, dtype=jnp.int32)[None, None, :]
    time = ((chip + other) % chips) * 2 * local_times + ((core + 1 + half) % 2) * local_times + step
    time = time.reshape(2, chips * local_times)
    freqs = jnp.arange(total_times, dtype=jnp.int32)
    lanes = jnp.arange(total_times * BAND, dtype=jnp.int32) // BAND
    weights = jnp.repeat(grid_weights, BAND)
    table = weights * jnp.cos(
        jnp.pi * (time[:, :, None].astype(jnp.float32) + 0.5) * lanes.astype(jnp.float32) / total_times
    )
    gains = jnp.sum(jnp.where(time[:, :, None, None] == freqs[:, None], greens, 0.0), axis=2)
    gains = jnp.repeat(gains, targets, axis=2)

    slabs[0][1], pieces = lax.optimization_barrier((slabs[0][1], pieces))
    timed = transform(pieces, spread_table(table))
    run = functools.partial(contract, timed=timed, gains=gains, dense=dense, owners=aux_count)
    swap = [(f, f ^ 1) for f in range(freq_count)]
    jobs = ((0, 0, chips), (1, 1, chips - 1), (1, 0, 1))
    totals = list(run(jobs, 0, slabs=slabs[0], totals=[], dtypes=(jnp.float32,) * 3))
    (given,) = run(jobs[:1], 1, slabs=slabs[1], totals=totals[:1], dtypes=(jnp.bfloat16,))
    taken = lax.ppermute(given, "freq", swap)
    (kept,) = run(jobs[1:2], 1, slabs=slabs[1], totals=totals[1:2], dtypes=(jnp.float32,))
    sent = [
        (kept[i - 1] + taken[i].astype(jnp.float32)).astype(jnp.bfloat16) for i in range(1, chips)
    ]

    def chip_shift(by):
        return [(2 * x + c, 2 * ((x + by) % chips) + c) for x in range(chips) for c in range(2)]

    totals[2], sent[0] = lax.optimization_barrier((totals[2], sent[0]))
    arrived = [lax.ppermute(sent[i], "freq", chip_shift(i + 1)) for i in range(chips - 1)]
    (kept,) = run(jobs[2:], 1, slabs=slabs[1], totals=totals[2:], dtypes=(jnp.float32,))
    summed = kept[0] + taken[0].astype(jnp.float32)
    for piece in arrived:
        summed = summed + piece.astype(jnp.float32)
    spread = lax.all_to_all(summed.astype(jnp.bfloat16), "aux", split_axis=0, concat_axis=0, tiled=True)
    return jnp.sum(spread.astype(jnp.float32), axis=0)


def solution(mesh):
    return jax.shard_map(
        shards,
        mesh=mesh,
        in_specs=(
            P("freq", "aux", None),
            P(),
            P(),
            P("aux", None, None),
            P("aux", None, None),
            P("aux", None),
            P("aux"),
            P(),
        ),
        out_specs=P("freq", "aux", None),
        check_vma=False,
    )
```

```python
import functools

import jax
import jax.numpy as jnp
from jax import lax
from jax.experimental import pallas as pl
from jax.experimental.pallas import tpu as pltpu
from jax.sharding import PartitionSpec as P

BAND = 16
DEPTH = 8
SHIFTS = ((0, 4, 3, 5, 2, 6, 1, 7), (0, 4, 1, 7, 2, 6, 3, 5))
WHOLE = pl.BlockSpec(memory_space=pltpu.VMEM)


def params(mebibytes=24):
    return pltpu.CompilerParams(vmem_limit_bytes=mebibytes * 1024 * 1024)


def pick_kernel(place_ref, screened_ref, out_ref, piece_ref, sems):
    place = place_ref[0]
    row, column = place // DEPTH, place % DEPTH
    odd = column % 2
    slab = out_ref.shape[3] // 4
    copies = []
    for f in range(out_ref.shape[0]):
        far = lax.rem(column + jnp.where(odd == 1, SHIFTS[1][f], SHIFTS[0][f]), DEPTH)
        for i in range(4):
            start = (lax.rem(row + i, 4) * DEPTH + far) * slab
            piece_ref[f, :, :, i * slab : (i + 1) * slab] = screened_ref[:, :, pl.ds(pl.multiple_of(start, slab), slab)]
        copies.append(pltpu.make_async_copy(piece_ref.at[f], out_ref.at[f], sems.at[f]))
        copies[-1].start()
    for copy in copies:
        copy.wait()


def pick(place, screened, freqs):
    local, rows, width = screened.shape
    shape = (freqs, local, rows, width // freqs)
    return pl.pallas_call(
        pick_kernel,
        out_shape=jax.ShapeDtypeStruct(shape, screened.dtype),
        in_specs=[pl.BlockSpec(memory_space=pltpu.SMEM), WHOLE],
        out_specs=pl.BlockSpec(memory_space=pl.ANY),
        scratch_shapes=[pltpu.VMEM(shape, screened.dtype), pltpu.SemaphoreType.DMA((freqs,))],
        compiler_params=params(16),
    )(place, screened)


def spread_kernel(table_ref, out_ref):
    times, wide = table_ref.shape[1:]
    lane = lax.broadcasted_iota(jnp.int32, (BAND, wide), 1) % BAND
    keep = lane == lax.broadcasted_iota(jnp.int32, (BAND, wide), 0)
    tall = times * BAND
    for half in range(2):
        for time in range(times):
            value = jnp.where(keep, table_ref[half, time : time + 1, :], 0.0)
            upper = value.astype(jnp.bfloat16)
            lower = (value - upper.astype(jnp.float32)).astype(jnp.bfloat16)
            out_ref[half, time * BAND : (time + 1) * BAND, :] = upper
            out_ref[half, tall + time * BAND : tall + (time + 1) * BAND, :] = lower


def spread_table(table):
    _, times, wide = table.shape
    return pl.pallas_call(
        spread_kernel,
        out_shape=jax.ShapeDtypeStruct((2, 2 * times * BAND, wide), jnp.bfloat16),
        in_specs=[WHOLE],
        out_specs=WHOLE,
        compiler_params=params(),
    )(table)


def mix_bands(pieces_ref, pieces_at, mix_ref, timed_ref):
    sources, local, rows, width = pieces_ref.shape
    places = timed_ref.shape[1]
    pair = 2 * BAND
    tall = places * pair
    bands = rows // BAND
    mix = mix_ref[...].reshape(4 * tall, sources * local * BAND)
    for band in range(bands):
        if band % 2 == 0:
            pieces_at[band // 2].wait()
        piece = pieces_ref[:, :, band * BAND : (band + 1) * BAND, :].reshape(sources * local * BAND, width)
        both = jnp.dot(mix, piece, preferred_element_type=jnp.float32)
        for half in range(2):
            upper = both[2 * half * tall : (2 * half + 1) * tall]
            lower = both[(2 * half + 1) * tall : (2 * half + 2) * tall]
            mixed = (upper + lower).astype(jnp.bfloat16)
            for place in range(places):
                timed_ref[half, place, band * pair : (band + 1) * pair, :] = mixed[place * pair : (place + 1) * pair]


def run_jobs(jobs, part, timed_ref, gains_ref, dense_ref, dense_at, state_ref, scaled_ref, totals, outs):
    span = state_ref.shape[1]
    blocks = dense_ref.shape[0]
    deep = scaled_ref.shape[0] // blocks
    tall, depth = timed_ref.shape[2:]
    bands = tall // (2 * BAND)
    bands_in = bands // blocks
    row_block = bands_in * BAND
    owners, inner, targets = outs[0].shape[1], outs[0].shape[3], outs[0].shape[4]
    pair = 2 * targets

    for number, ((half, first, count), total_ref, out_ref) in enumerate(zip(jobs, totals, outs)):
        timed = timed_ref[half, first : first + count].reshape(count * tall, depth)

        def states(step, carry):
            columns = pl.ds(pl.multiple_of(step * pair, pair), pair)
            contracted = jnp.dot(timed, state_ref[:, columns], preferred_element_type=jnp.float32)
            gains = gains_ref[half, :, pl.ds(pl.multiple_of(part * span + step * pair, pair), pair)]
            for place in range(count):
                for time in range(2):
                    at = 2 * (first + place) + time
                    gain = gains[at : at + 1, :]
                    column = (2 * place + time) * targets
                    for band in range(bands):
                        row = place * tall + (2 * band + time) * BAND
                        block = (contracted[row : row + BAND, :] * gain).astype(jnp.bfloat16)
                        base = (band // bands_in) * deep + (band % bands_in) * BAND
                        for state in range(2):
                            start = pl.multiple_of(base + (step * 2 + state) * row_block, BAND)
                            scaled_ref[pl.ds(start, BAND), column : column + targets] = block[
                                :, state * targets : (state + 1) * targets
                            ]
            return carry

        lax.fori_loop(0, span // pair, states, 0)
        if number == 0:
            dense_at.wait()
        for place in range(count):
            columns = slice(place * pair, (place + 1) * pair)
            value = sum(
                jnp.dot(
                    dense_ref[block],
                    scaled_ref[block * deep : (block + 1) * deep, columns],
                    preferred_element_type=jnp.float32,
                )
                for block in range(blocks)
            )
            for time in range(2):
                piece = value[:, time * targets : (time + 1) * targets].reshape(owners, inner, targets)
                if total_ref is not None:
                    piece = piece + total_ref[place, :, time, :, :]
                out_ref[place, :, time, :, :] = piece.astype(out_ref.dtype)


def first_kernel(jobs, *refs):
    pieces_in, mix_ref, gains_ref, dense_in = refs[:4]
    slabs, refs = refs[4:8], refs[8:]
    timed_ref, outs = refs[0], refs[1 : 1 + len(jobs)]
    pieces_ref, state_ref, scaled_ref, dense_ref, pieces_sem, slab_sem, dense_sem = refs[1 + len(jobs) :]
    deep = dense_ref.shape[2]
    pieces_at = []
    for i in range(pieces_sem.shape[0]):
        rows = pl.ds(i * 2 * BAND, 2 * BAND)
        pieces_at.append(pltpu.make_async_copy(pieces_in.at[:, :, rows], pieces_ref.at[:, :, rows], pieces_sem.at[i]))
        pieces_at[-1].start()
    slabs_at = slab_copies(slabs, state_ref, slab_sem)
    dense_at = pltpu.make_async_copy(dense_in.at[:, :, pl.ds(0, deep)], dense_ref, dense_sem.at[0])
    dense_at.start()
    mix_bands(pieces_ref, pieces_at, mix_ref, timed_ref)
    for copy in slabs_at:
        copy.wait()
    run_jobs(
        jobs, 0, timed_ref, gains_ref, dense_ref, dense_at, state_ref, scaled_ref, (None,) * len(jobs), outs
    )


def slab_copies(slabs, state_ref, slab_sem):
    slab = slabs[0].shape[0]
    copies = []
    for i in range(4):
        copies.append(pltpu.make_async_copy(slabs[i], state_ref.at[pl.ds(i * slab, slab)], slab_sem.at[i]))
        copies[-1].start()
    return copies


def last_kernel(job, gather, *refs):
    timed_ref, gains_ref, dense_in, total_ref = refs[:4]
    if gather:
        slabs, (out_ref, state_ref, scaled_ref, dense_ref, dense_sem, slab_sem) = refs[4:8], refs[8:]
        slabs_at = slab_copies(slabs, state_ref, slab_sem)
    else:
        state_ref, out_ref, scaled_ref, dense_ref, dense_sem = refs[4:]
    deep = dense_ref.shape[2]
    dense_at = pltpu.make_async_copy(dense_in.at[:, :, pl.ds(deep, deep)], dense_ref, dense_sem.at[0])
    dense_at.start()
    if gather:
        for copy in slabs_at:
            copy.wait()
    run_jobs(
        (job,), 1, timed_ref, gains_ref, dense_ref, dense_at, state_ref, scaled_ref, (total_ref,), (out_ref,)
    )


AWAY = pl.BlockSpec(memory_space=pl.ANY)


def sums_shape(count, dense, owners, targets, dtype):
    return jax.ShapeDtypeStruct((count, owners, 2, dense.shape[1] // owners, targets), dtype)


def cost(work, rows, depth, span, dense, targets):
    deep = span // targets * rows
    return pl.CostEstimate(
        flops=4 * work * (rows * depth * span + dense.shape[1] * deep * targets),
        bytes_accessed=2 * 1024 * 1024 * work,
        transcendentals=0,
    )


def first_part(jobs, pieces, mix, gains, dense, slabs, owners):
    sources, local, rows, width = pieces.shape
    slab, span = slabs[0].shape
    blocks = dense.shape[0]
    targets = gains.shape[2] // (blocks * dense.shape[2] // rows)
    times = gains.shape[1]
    depth = span // targets * rows
    wide = max(count for _, _, count in jobs)
    return pl.pallas_call(
        functools.partial(first_kernel, jobs),
        out_shape=[jax.ShapeDtypeStruct((2, times // 2, 2 * rows, width), jnp.bfloat16)]
        + [sums_shape(count, dense, owners, targets, jnp.float32) for _, _, count in jobs],
        in_specs=[AWAY, WHOLE, WHOLE, AWAY] + [AWAY] * 4,
        out_specs=[WHOLE] * (1 + len(jobs)),
        scratch_shapes=[
            pltpu.VMEM(pieces.shape, jnp.bfloat16),
            pltpu.VMEM((4 * slab, span), jnp.bfloat16),
            pltpu.VMEM((depth, wide * 2 * targets), jnp.bfloat16),
            pltpu.VMEM((blocks, dense.shape[1], depth // blocks), jnp.bfloat16),
            pltpu.SemaphoreType.DMA((rows // (2 * BAND),)),
            pltpu.SemaphoreType.DMA((4,)),
            pltpu.SemaphoreType.DMA((1,)),
        ],
        compiler_params=params(),
        cost_estimate=cost(sum(count for _, _, count in jobs), rows, 4 * slab, span, dense, targets),
    )(pieces, mix, gains, dense, *slabs)


def last_part(job, timed, gains, dense, state, total, dtype, owners):
    gather = isinstance(state, list)
    slabs = state if gather else []
    span = slabs[0].shape[1] if gather else state.shape[1]
    depth_in = timed.shape[3]
    rows = timed.shape[2] // 2
    blocks = dense.shape[0]
    targets = gains.shape[2] // (blocks * dense.shape[2] // rows)
    depth = span // targets * rows
    count = job[2]
    out_shape = [sums_shape(count, dense, owners, targets, dtype)]
    scratch = [
        pltpu.VMEM((depth, count * 2 * targets), jnp.bfloat16),
        pltpu.VMEM((blocks, dense.shape[1], depth // blocks), jnp.bfloat16),
        pltpu.SemaphoreType.DMA((1,)),
    ]
    if gather:
        out_shape.append(jax.ShapeDtypeStruct((depth_in, span), jnp.bfloat16))
        scratch.append(pltpu.SemaphoreType.DMA((4,)))
    operands = [timed, gains, dense, total] + (slabs if gather else [state])
    return pl.pallas_call(
        functools.partial(last_kernel, job, gather),
        out_shape=out_shape,
        in_specs=[WHOLE, WHOLE, AWAY, WHOLE] + ([AWAY] * 4 if gather else [WHOLE]),
        out_specs=[WHOLE] * len(out_shape),
        scratch_shapes=scratch,
        compiler_params=params(),
        cost_estimate=cost(count, rows, depth_in, span, dense, targets),
    )(*operands)


def shards(
    screened, grid_weights, greens, three_state, three_orbital, block_ids, block_counts, owners
):
    freq_count = lax.axis_size("freq")
    aux_count = lax.axis_size("aux")
    freq = lax.axis_index("freq")
    chip, core = freq // 2, freq % 2
    local_times, rows, width = screened.shape
    total_times = local_times * freq_count
    states = three_state.shape[1]
    targets = three_state.shape[2]
    block_count, slot_count = block_ids.shape
    orbitals = three_orbital.shape[2]
    block_width = orbitals // slot_count
    row_block = rows // block_count
    chips = freq_count // 2
    height = aux_count // DEPTH

    along = []
    for f in range(freq_count):
        for y in range(height):
            for z in range(DEPTH):
                far = (z + SHIFTS[z % 2][f]) % DEPTH
                along.append((f * aux_count + y * DEPTH + far, f * aux_count + y * DEPTH + z))
    across = [
        [(((y + i) % height) * DEPTH + z, y * DEPTH + z) for y in range(height) for z in range(DEPTH)]
        for i in range(height)
    ]
    flat_state = three_state.reshape(rows, states * targets)
    flat_state, screened = lax.optimization_barrier((flat_state, screened))
    span = states * targets // 2
    first, second = (flat_state[:, part * span : (part + 1) * span] for part in range(2))
    own = lax.ppermute(first, ("freq", "aux"), along)
    far = lax.ppermute(second, "aux", across[2])
    own, far = lax.optimization_barrier((own, far))
    slabs = [[own] + [lax.ppermute(own, "aux", across[i]) for i in range(1, height)]]
    second, far, slabs[0][1] = lax.optimization_barrier((second, far, slabs[0][1]))
    own = lax.ppermute(second, ("freq", "aux"), along)
    far = lax.ppermute(far, ("freq", "aux"), along)
    slabs.append([own, None, far, None])
    for i in (1, 3):
        ready, slabs[0][i] = lax.optimization_barrier((own, slabs[0][i]))
        slabs[1][i] = lax.ppermute(ready, "aux", across[i])

    device = jnp.arange(aux_count, dtype=jnp.int32)
    owned = jnp.sum(jnp.where(owners[None, :] == device[:, None], device[None, :], 0), axis=1)
    inner = orbitals // aux_count
    wanted = (owned[:, None] * inner + jnp.arange(inner, dtype=jnp.int32)[None, :]).reshape(orbitals)
    slot = jnp.arange(slot_count, dtype=jnp.int32)
    listed = block_ids[:, :, None] * block_width + jnp.arange(block_width, dtype=jnp.int32)
    listed = jnp.where(slot[None, :, None] < block_counts[:, None, None], listed, -1).reshape(block_count, orbitals)
    choose = (wanted[None, :, None] == listed[:, None, :]).astype(jnp.bfloat16)
    _, three_orbital = lax.optimization_barrier((slabs[0][1], three_orbital))
    values = three_orbital.reshape(block_count, row_block, states, orbitals)
    values = values.transpose(0, 2, 1, 3).reshape(block_count, states * row_block, orbitals)
    dense = jnp.einsum("bns,brs->bnr", choose, values, preferred_element_type=jnp.float32).astype(jnp.bfloat16)
    place = lax.axis_index("aux").astype(jnp.int32).reshape(1)
    pieces = pick(place, screened, freq_count)
    pieces = lax.all_to_all(pieces, "freq", split_axis=0, concat_axis=0, tiled=True)

    half = jnp.arange(2, dtype=jnp.int32)[:, None, None]
    other = jnp.arange(chips, dtype=jnp.int32)[None, :, None]
    step = jnp.arange(local_times, dtype=jnp.int32)[None, None, :]
    time = ((chip + other) % chips) * 2 * local_times + ((core + 1 + half) % 2) * local_times + step
    time = time.reshape(2, chips * local_times)
    freqs = jnp.arange(total_times, dtype=jnp.int32)
    lanes = jnp.arange(total_times * BAND, dtype=jnp.int32) // BAND
    weights = jnp.repeat(grid_weights, BAND)
    table = weights * jnp.cos(
        jnp.pi * (time[:, :, None].astype(jnp.float32) + 0.5) * lanes.astype(jnp.float32) / total_times
    )
    gains = jnp.sum(jnp.where(time[:, :, None, None] == freqs[:, None], greens, 0.0), axis=2)
    gains = jnp.repeat(gains, targets, axis=2)

    swap = [(f, f ^ 1) for f in range(freq_count)]
    jobs = ((0, 0, chips), (1, 1, chips - 1), (1, 0, 1))
    timed, *totals = first_part(jobs, pieces, spread_table(table), gains, dense, slabs[0], aux_count)
    run = functools.partial(last_part, timed=timed, gains=gains, dense=dense, owners=aux_count)
    given, state = run(jobs[0], state=slabs[1], total=totals[0], dtype=jnp.bfloat16)
    taken = lax.ppermute(given, "freq", swap)
    (kept,) = run(jobs[1], state=state, total=totals[1], dtype=jnp.float32)
    sent = [
        (kept[i - 1] + taken[i].astype(jnp.float32)).astype(jnp.bfloat16) for i in range(1, chips)
    ]

    def chip_shift(by):
        return [(2 * x + c, 2 * ((x + by) % chips) + c) for x in range(chips) for c in range(2)]

    totals[2], sent[0] = lax.optimization_barrier((totals[2], sent[0]))
    arrived = [lax.ppermute(sent[i], "freq", chip_shift(i + 1)) for i in range(chips - 1)]
    (kept,) = run(jobs[2], state=state, total=totals[2], dtype=jnp.float32)
    summed = kept[0] + taken[0].astype(jnp.float32)
    for piece in arrived:
        summed = summed + piece.astype(jnp.float32)
    spread = lax.all_to_all(summed.astype(jnp.bfloat16), "aux", split_axis=0, concat_axis=0, tiled=True)
    return jnp.sum(spread.astype(jnp.float32), axis=0)


def solution(mesh):
    return jax.shard_map(
        shards,
        mesh=mesh,
        in_specs=(
            P("freq", "aux", None),
            P(),
            P(),
            P("aux", None, None),
            P("aux", None, None),
            P("aux", None),
            P("aux"),
            P(),
        ),
        out_specs=P("freq", "aux", None),
        check_vma=False,
    )
```

```python
import functools

import jax
import jax.numpy as jnp
from jax import lax
from jax.experimental import pallas as pl
from jax.experimental.pallas import tpu as pltpu
from jax.sharding import PartitionSpec as P

BAND = 16
DEPTH = 8
SHIFTS = ((0, 4, 3, 5, 2, 6, 1, 7), (0, 4, 1, 7, 2, 6, 3, 5))
WHOLE = pl.BlockSpec(memory_space=pltpu.VMEM)


def params(mebibytes=24):
    return pltpu.CompilerParams(vmem_limit_bytes=mebibytes * 1024 * 1024)


def pick_kernel(place_ref, freq_ref, shifts_ref, screened_ref, *refs):
    count = len(refs) - 2
    outs, piece_ref, sems = refs[:count], refs[count], refs[count + 1]
    place, freq = place_ref[0], freq_ref[0]
    row, column = place // DEPTH, place % DEPTH
    slab = outs[0].shape[2] // 4
    copies = []
    for r in range(count):
        target = lax.rem(freq // 2 + r // 2, count // 2) * 2 + lax.rem(freq + r, 2)
        far = lax.rem(column + shifts_ref[lax.rem(column, 2) * count + target], DEPTH)
        for i in range(4):
            start = (lax.rem(row + i, 4) * DEPTH + far) * slab
            piece_ref[r, :, :, i * slab : (i + 1) * slab] = screened_ref[:, :, pl.ds(pl.multiple_of(start, slab), slab)]
        copies.append(pltpu.make_async_copy(piece_ref.at[r], outs[r], sems.at[r]))
        copies[-1].start()
    for copy in copies:
        copy.wait()


def pick(place, freq, screened, freqs):
    local, rows, width = screened.shape
    shape = (local, rows, width // freqs)
    shifts = jnp.array(SHIFTS, dtype=jnp.int32).reshape(2 * freqs)
    return pl.pallas_call(
        pick_kernel,
        out_shape=[jax.ShapeDtypeStruct(shape, screened.dtype)] * freqs,
        in_specs=[pl.BlockSpec(memory_space=pltpu.SMEM)] * 3 + [WHOLE],
        out_specs=[pl.BlockSpec(memory_space=pl.ANY)] * freqs,
        scratch_shapes=[pltpu.VMEM((freqs, *shape), screened.dtype), pltpu.SemaphoreType.DMA((freqs,))],
        compiler_params=params(16),
    )(place, freq, shifts, screened)


def dense_kernel(owners_ref, ids_ref, counts_ref, values_ref, out_ref):
    blocks, orbitals, _ = out_ref.shape
    aux, slots = owners_ref.shape[0], ids_ref.shape[1]
    inner, block_width = orbitals // aux, orbitals // slots
    row = lax.broadcasted_iota(jnp.int32, (orbitals, 128), 0)
    owned = jnp.zeros((orbitals, 128), jnp.int32)
    for g in range(aux):
        owned = jnp.where(row // inner == owners_ref[g], g, owned)
    wanted = (owned * inner + row % inner)[:, :1]
    lane = lax.broadcasted_iota(jnp.int32, (8, orbitals), 1)
    for block in range(blocks):
        listed = jnp.full((8, orbitals), -1, jnp.int32)
        for s in range(slots):
            used = (lane // block_width == s) & (s < counts_ref[block])
            listed = jnp.where(used, ids_ref[block, s] * block_width + lane % block_width, listed)
        choose = jnp.where(wanted == listed[:1], 1.0, 0.0).astype(jnp.bfloat16)
        out_ref[block] = lax.dot_general(
            choose, values_ref[block], (((1,), (1,)), ((), ())), preferred_element_type=jnp.float32
        ).astype(jnp.bfloat16)


def expand(owners, block_ids, block_counts, values):
    blocks, rows, orbitals = values.shape
    return pl.pallas_call(
        dense_kernel,
        out_shape=jax.ShapeDtypeStruct((blocks, orbitals, rows), jnp.bfloat16),
        in_specs=[pl.BlockSpec(memory_space=pltpu.SMEM)] * 3 + [WHOLE],
        out_specs=WHOLE,
        compiler_params=params(16),
    )(owners, block_ids, block_counts, values)


def spread_kernel(table_ref, out_ref):
    times, wide = table_ref.shape[1:]
    lane = lax.broadcasted_iota(jnp.int32, (BAND, wide), 1) % BAND
    keep = lane == lax.broadcasted_iota(jnp.int32, (BAND, wide), 0)
    tall = times * BAND
    for half in range(2):
        for time in range(times):
            value = jnp.where(keep, table_ref[half, time : time + 1, :], 0.0)
            upper = value.astype(jnp.bfloat16)
            lower = (value - upper.astype(jnp.float32)).astype(jnp.bfloat16)
            out_ref[half, time * BAND : (time + 1) * BAND, :] = upper
            out_ref[half, tall + time * BAND : tall + (time + 1) * BAND, :] = lower


def spread_table(table):
    _, times, wide = table.shape
    return pl.pallas_call(
        spread_kernel,
        out_shape=jax.ShapeDtypeStruct((2, 2 * times * BAND, wide), jnp.bfloat16),
        in_specs=[WHOLE],
        out_specs=WHOLE,
        compiler_params=params(),
    )(table)


def mix_bands(pieces_ref, pieces_at, mix_ref, timed_ref):
    sources, local, rows, width = pieces_ref.shape
    places = timed_ref.shape[1]
    pair = 2 * BAND
    tall = places * pair
    bands = rows // BAND
    mix = mix_ref[...].reshape(4 * tall, sources * local * BAND)
    for band in range(bands):
        if band % 2 == 0:
            for copy in pieces_at[band // 2]:
                copy.wait()
        piece = pieces_ref[:, :, band * BAND : (band + 1) * BAND, :].reshape(sources * local * BAND, width)
        both = jnp.dot(mix, piece, preferred_element_type=jnp.float32)
        for half in range(2):
            upper = both[2 * half * tall : (2 * half + 1) * tall]
            lower = both[(2 * half + 1) * tall : (2 * half + 2) * tall]
            mixed = (upper + lower).astype(jnp.bfloat16)
            for place in range(places):
                timed_ref[half, place, band * pair : (band + 1) * pair, :] = mixed[place * pair : (place + 1) * pair]


def run_jobs(jobs, part, timed_ref, gains_ref, dense_ref, state_ref, scaled_ref, totals, outs):
    span = state_ref.shape[1]
    blocks = dense_ref.shape[0]
    deep = scaled_ref.shape[0] // blocks
    tall, depth = timed_ref.shape[2:]
    bands = tall // (2 * BAND)
    bands_in = bands // blocks
    row_block = bands_in * BAND
    owners, inner, targets = outs[0].shape[1], outs[0].shape[3], outs[0].shape[4]
    pair = 2 * targets

    for (half, first, count), total_ref, out_ref in zip(jobs, totals, outs):
        timed = timed_ref[half, first : first + count].reshape(count * tall, depth)

        def states(step, carry):
            columns = pl.ds(pl.multiple_of(step * pair, pair), pair)
            contracted = jnp.dot(timed, state_ref[:, columns], preferred_element_type=jnp.float32)
            gains = gains_ref[half, :, pl.ds(pl.multiple_of(part * span + step * pair, pair), pair)]
            for place in range(count):
                for time in range(2):
                    at = 2 * (first + place) + time
                    gain = gains[at : at + 1, :]
                    column = (2 * place + time) * targets
                    for band in range(bands):
                        row = place * tall + (2 * band + time) * BAND
                        block = (contracted[row : row + BAND, :] * gain).astype(jnp.bfloat16)
                        base = (band // bands_in) * deep + (band % bands_in) * BAND
                        for state in range(2):
                            start = pl.multiple_of(base + (step * 2 + state) * row_block, BAND)
                            scaled_ref[pl.ds(start, BAND), column : column + targets] = block[
                                :, state * targets : (state + 1) * targets
                            ]
            return carry

        lax.fori_loop(0, span // pair, states, 0)
        for place in range(count):
            columns = slice(place * pair, (place + 1) * pair)
            value = sum(
                jnp.dot(
                    dense_ref[block, :, part * deep : (part + 1) * deep],
                    scaled_ref[block * deep : (block + 1) * deep, columns],
                    preferred_element_type=jnp.float32,
                )
                for block in range(blocks)
            )
            for time in range(2):
                piece = value[:, time * targets : (time + 1) * targets].reshape(owners, inner, targets)
                if total_ref is not None:
                    piece = piece + total_ref[place, :, time, :, :]
                out_ref[place, :, time, :, :] = piece.astype(out_ref.dtype)


def first_kernel(jobs, sources, *refs):
    pieces, refs = refs[:sources], refs[sources:]
    mix_ref, gains_ref, dense_ref = refs[:3]
    slabs, refs = refs[3:7], refs[7:]
    timed_ref, outs = refs[0], refs[1 : 1 + len(jobs)]
    pieces_ref, state_ref, scaled_ref, pieces_sem, slab_sem = refs[1 + len(jobs) :]
    pieces_at = []
    for i in range(pieces_sem.shape[0]):
        rows = pl.ds(i * 2 * BAND, 2 * BAND)
        copies = []
        for r in range(sources):
            copies.append(
                pltpu.make_async_copy(pieces[r].at[:, rows], pieces_ref.at[r, :, rows], pieces_sem.at[i, r])
            )
            copies[-1].start()
        pieces_at.append(copies)
    slab = slabs[0].shape[0]
    slabs_at = []
    for i in range(4):
        slabs_at.append(pltpu.make_async_copy(slabs[i], state_ref.at[pl.ds(i * slab, slab)], slab_sem.at[i]))
        slabs_at[-1].start()
    mix_bands(pieces_ref, pieces_at, mix_ref, timed_ref)
    for copy in slabs_at:
        copy.wait()
    run_jobs(jobs, 0, timed_ref, gains_ref, dense_ref, state_ref, scaled_ref, (None,) * len(jobs), outs)


def last_kernel(job, gather, *refs):
    timed_ref, gains_ref, dense_ref, total_ref = refs[:4]
    if gather:
        slabs, (out_ref, state_ref, scaled_ref) = refs[4:8], refs[8:]
        slab = slabs[0].shape[0]
        for i in range(4):
            state_ref[i * slab : (i + 1) * slab, :] = slabs[i][...]
    else:
        state_ref, out_ref, scaled_ref = refs[4:]
    run_jobs((job,), 1, timed_ref, gains_ref, dense_ref, state_ref, scaled_ref, (total_ref,), (out_ref,))


AWAY = pl.BlockSpec(memory_space=pl.ANY)


def sums_shape(count, dense, owners, targets, dtype):
    return jax.ShapeDtypeStruct((count, owners, 2, dense.shape[1] // owners, targets), dtype)


def cost(work, rows, depth, span, dense, targets):
    deep = span // targets * rows
    return pl.CostEstimate(
        flops=4 * work * (rows * depth * span + dense.shape[1] * deep * targets),
        bytes_accessed=2 * 1024 * 1024 * work,
        transcendentals=0,
    )


def first_part(jobs, pieces, mix, gains, dense, slabs, owners):
    local, rows, width = pieces[0].shape
    slab, span = slabs[0].shape
    blocks = dense.shape[0]
    targets = gains.shape[2] // (blocks * dense.shape[2] // rows)
    times = gains.shape[1]
    depth = span // targets * rows
    wide = max(count for _, _, count in jobs)
    return pl.pallas_call(
        functools.partial(first_kernel, jobs, len(pieces)),
        out_shape=[jax.ShapeDtypeStruct((2, times // 2, 2 * rows, width), jnp.bfloat16)]
        + [sums_shape(count, dense, owners, targets, jnp.float32) for _, _, count in jobs],
        in_specs=[AWAY] * len(pieces) + [WHOLE] * 3 + [AWAY] * 4,
        out_specs=[WHOLE] * (1 + len(jobs)),
        scratch_shapes=[
            pltpu.VMEM((len(pieces), local, rows, width), jnp.bfloat16),
            pltpu.VMEM((4 * slab, span), jnp.bfloat16),
            pltpu.VMEM((depth, wide * 2 * targets), jnp.bfloat16),
            pltpu.SemaphoreType.DMA((rows // (2 * BAND), len(pieces))),
            pltpu.SemaphoreType.DMA((4,)),
        ],
        compiler_params=params(),
        cost_estimate=cost(sum(count for _, _, count in jobs), rows, 4 * slab, span, dense, targets),
    )(*pieces, mix, gains, dense, *slabs)


def last_part(job, timed, gains, dense, state, total, dtype, owners):
    gather = isinstance(state, list)
    slabs = state if gather else [state]
    span = slabs[0].shape[1]
    depth_in = timed.shape[3]
    rows = timed.shape[2] // 2
    blocks = dense.shape[0]
    targets = gains.shape[2] // (blocks * dense.shape[2] // rows)
    depth = span // targets * rows
    count = job[2]
    out_shape = [sums_shape(count, dense, owners, targets, dtype)]
    if gather:
        out_shape.append(jax.ShapeDtypeStruct((depth_in, span), jnp.bfloat16))
    operands = [timed, gains, dense, total, *slabs]
    return pl.pallas_call(
        functools.partial(last_kernel, job, gather),
        out_shape=out_shape,
        in_specs=[WHOLE] * len(operands),
        out_specs=[WHOLE] * len(out_shape),
        scratch_shapes=[pltpu.VMEM((depth, count * 2 * targets), jnp.bfloat16)],
        compiler_params=params(),
        cost_estimate=cost(count, rows, depth_in, span, dense, targets),
    )(*operands)


def shards(
    screened, grid_weights, greens, three_state, three_orbital, block_ids, block_counts, owners
):
    freq_count = lax.axis_size("freq")
    aux_count = lax.axis_size("aux")
    freq = lax.axis_index("freq")
    chip, core = freq // 2, freq % 2
    local_times, rows, width = screened.shape
    total_times = local_times * freq_count
    states = three_state.shape[1]
    targets = three_state.shape[2]
    block_count, slot_count = block_ids.shape
    orbitals = three_orbital.shape[2]
    block_width = orbitals // slot_count
    row_block = rows // block_count
    chips = freq_count // 2
    height = aux_count // DEPTH

    along = []
    for f in range(freq_count):
        for y in range(height):
            for z in range(DEPTH):
                far = (z + SHIFTS[z % 2][f]) % DEPTH
                along.append((f * aux_count + y * DEPTH + far, f * aux_count + y * DEPTH + z))
    across = [
        [(((y + i) % height) * DEPTH + z, y * DEPTH + z) for y in range(height) for z in range(DEPTH)]
        for i in range(height)
    ]
    flat_state = three_state.reshape(rows, states * targets)
    span = states * targets // 2
    first, second = (flat_state[:, part * span : (part + 1) * span] for part in range(2))
    first, second, screened = lax.optimization_barrier((first, second, screened))
    own = lax.ppermute(first, ("freq", "aux"), along)
    far = lax.ppermute(second, "aux", across[2])
    own, far = lax.optimization_barrier((own, far))
    slabs = [[own] + [lax.ppermute(own, "aux", across[i]) for i in range(1, height)]]
    second, far, slabs[0][1] = lax.optimization_barrier((second, far, slabs[0][1]))
    own = lax.ppermute(second, ("freq", "aux"), along)
    far = lax.ppermute(far, ("freq", "aux"), along)
    slabs.append([own, None, far, None])
    for i in (1, 3):
        ready, slabs[0][i] = lax.optimization_barrier((own, slabs[0][i]))
        slabs[1][i] = lax.ppermute(ready, "aux", across[i])

    _, three_orbital = lax.optimization_barrier((slabs[0][1], three_orbital))
    values = three_orbital.reshape(block_count, row_block, states, orbitals)
    values = values.transpose(0, 2, 1, 3).reshape(block_count, states * row_block, orbitals)
    dense = expand(owners, block_ids, block_counts, values)

    place = lax.axis_index("aux").astype(jnp.int32).reshape(1)
    pieces = list(pick(place, freq.astype(jnp.int32).reshape(1), screened, freq_count))
    for r in (2, 6, 4, 5, 3, 7, 1):
        moves = [(f, (f // 2 + r // 2) % chips * 2 + (f + r) % 2) for f in range(freq_count)]
        pieces[r] = lax.ppermute(pieces[r], "freq", moves)

    half = jnp.arange(2, dtype=jnp.int32)[:, None, None]
    other = jnp.arange(chips, dtype=jnp.int32)[None, :, None]
    step = jnp.arange(local_times, dtype=jnp.int32)[None, None, :]
    time = ((chip + other) % chips) * 2 * local_times + ((core + 1 + half) % 2) * local_times + step
    time = time.reshape(2, chips * local_times)
    freqs = jnp.arange(total_times, dtype=jnp.int32)
    lane = jnp.arange(total_times * BAND, dtype=jnp.int32) // BAND
    away = lane // local_times
    source = (chip + chips - away // 2) % chips * 2 + (core + away) % 2
    lanes = source * local_times + lane % local_times
    weights = jnp.sum(jnp.where(lanes[:, None] == freqs, grid_weights, 0.0), axis=1)
    table = weights * jnp.cos(
        jnp.pi * (time[:, :, None].astype(jnp.float32) + 0.5) * lanes.astype(jnp.float32) / total_times
    )
    gains = jnp.sum(jnp.where(time[:, :, None, None] == freqs[:, None], greens, 0.0), axis=2)
    gains = jnp.repeat(gains, targets, axis=2)

    swap = [(f, f ^ 1) for f in range(freq_count)]
    jobs = ((0, 0, chips), (1, 1, chips - 1), (1, 0, 1))
    timed, *totals = first_part(jobs, pieces, spread_table(table), gains, dense, slabs[0], aux_count)
    run = functools.partial(last_part, timed=timed, gains=gains, dense=dense, owners=aux_count)
    given, state = run(jobs[0], state=slabs[1], total=totals[0], dtype=jnp.bfloat16)
    taken = lax.ppermute(given, "freq", swap)
    (kept,) = run(jobs[1], state=state, total=totals[1], dtype=jnp.float32)
    sent = [
        (kept[i - 1] + taken[i].astype(jnp.float32)).astype(jnp.bfloat16) for i in range(1, chips)
    ]

    def chip_shift(by):
        return [(2 * x + c, 2 * ((x + by) % chips) + c) for x in range(chips) for c in range(2)]

    totals[2], sent[0] = lax.optimization_barrier((totals[2], sent[0]))
    arrived = [lax.ppermute(sent[i], "freq", chip_shift(i + 1)) for i in range(chips - 1)]
    (kept,) = run(jobs[2], state=state, total=totals[2], dtype=jnp.float32)
    summed = kept[0] + taken[0].astype(jnp.float32)
    for piece in arrived:
        summed = summed + piece.astype(jnp.float32)
    spread = lax.all_to_all(summed.astype(jnp.bfloat16), "aux", split_axis=0, concat_axis=0, tiled=True)
    return jnp.sum(spread.astype(jnp.float32), axis=0)


def solution(mesh):
    return jax.shard_map(
        shards,
        mesh=mesh,
        in_specs=(
            P("freq", "aux", None),
            P(),
            P(),
            P("aux", None, None),
            P("aux", None, None),
            P("aux", None),
            P("aux"),
            P(),
        ),
        out_specs=P("freq", "aux", None),
        check_vma=False,
    )
```

```python
import functools

import jax
import jax.numpy as jnp
from jax import lax
from jax.experimental import pallas as pl
from jax.experimental.pallas import tpu as pltpu
from jax.sharding import PartitionSpec as P

BAND = 16
DEPTH = 8
SHIFTS = ((0, 4, 3, 5, 2, 6, 1, 7), (0, 4, 1, 7, 2, 6, 3, 5))
ORDER = (0, 2, 1, 3)
WHOLE = pl.BlockSpec(memory_space=pltpu.VMEM)


def params(mebibytes=32):
    return pltpu.CompilerParams(vmem_limit_bytes=mebibytes * 1024 * 1024)


def pick_kernel(place_ref, screened_ref, out_ref, piece_ref, sems):
    place = place_ref[0]
    row, column = place // DEPTH, place % DEPTH
    odd = column % 2
    slab = out_ref.shape[3] // 4
    copies = []
    for f in range(out_ref.shape[0]):
        far = lax.rem(column + jnp.where(odd == 1, SHIFTS[1][f], SHIFTS[0][f]), DEPTH)
        for i in range(4):
            start = (lax.rem(row + i, 4) * DEPTH + far) * slab
            piece_ref[f, :, :, i * slab : (i + 1) * slab] = screened_ref[:, :, pl.ds(pl.multiple_of(start, slab), slab)]
        copies.append(pltpu.make_async_copy(piece_ref.at[f], out_ref.at[f], sems.at[f]))
        copies[-1].start()
    for copy in copies:
        copy.wait()


def pick(place, screened, freqs):
    local, rows, width = screened.shape
    shape = (freqs, local, rows, width // freqs)
    return pl.pallas_call(
        pick_kernel,
        out_shape=jax.ShapeDtypeStruct(shape, screened.dtype),
        in_specs=[pl.BlockSpec(memory_space=pltpu.SMEM), WHOLE],
        out_specs=pl.BlockSpec(memory_space=pl.ANY),
        scratch_shapes=[pltpu.VMEM(shape, screened.dtype), pltpu.SemaphoreType.DMA((freqs,))],
        compiler_params=params(16),
    )(place, screened)


def spread_kernel(table_ref, out_ref):
    times, wide = table_ref.shape[1:]
    lane = lax.broadcasted_iota(jnp.int32, (BAND, wide), 1) % BAND
    keep = lane == lax.broadcasted_iota(jnp.int32, (BAND, wide), 0)
    tall = times * BAND
    for half in range(2):
        for time in range(times):
            value = jnp.where(keep, table_ref[half, time : time + 1, :], 0.0)
            upper = value.astype(jnp.bfloat16)
            lower = (value - upper.astype(jnp.float32)).astype(jnp.bfloat16)
            out_ref[half, time * BAND : (time + 1) * BAND, :] = upper
            out_ref[half, tall + time * BAND : tall + (time + 1) * BAND, :] = lower


def spread_table(table):
    _, times, wide = table.shape
    return pl.pallas_call(
        spread_kernel,
        out_shape=jax.ShapeDtypeStruct((2, 2 * times * BAND, wide), jnp.bfloat16),
        in_specs=[WHOLE],
        out_specs=WHOLE,
        compiler_params=params(),
    )(table)


def mix_kernel(pieces_ref, mix_ref, out_ref):
    sources, local, rows, width = pieces_ref.shape
    freqs = sources * local
    places = out_ref.shape[1]
    pair = 2 * BAND
    tall = places * pair
    mix = mix_ref[...].reshape(4 * tall, freqs * BAND)
    for band in range(rows // BAND):
        piece = pieces_ref[:, :, band * BAND : (band + 1) * BAND, :].reshape(freqs * BAND, width)
        both = jnp.dot(mix, piece, preferred_element_type=jnp.float32)
        for half in range(2):
            upper = both[2 * half * tall : (2 * half + 1) * tall]
            lower = both[(2 * half + 1) * tall : (2 * half + 2) * tall]
            mixed = (upper + lower).astype(jnp.bfloat16)
            for place in range(places):
                out_ref[half, place, band * pair : (band + 1) * pair, :] = mixed[place * pair : (place + 1) * pair]


def transform(pieces, mix):
    sources, local, rows, width = pieces.shape
    times = mix.shape[1] // (2 * BAND)
    return pl.pallas_call(
        mix_kernel,
        out_shape=jax.ShapeDtypeStruct((2, times // 2, 2 * rows, width), jnp.bfloat16),
        in_specs=[WHOLE] * 2,
        out_specs=WHOLE,
        compiler_params=params(),
    )(pieces, mix)


def contract_kernel(jobs, part, has_total, *refs):
    timed_ref, gains_ref, dense_ref = refs[:3]
    slabs = refs[3:7]
    refs = refs[7:]
    totals = ()
    if has_total:
        totals, refs = refs[:2], refs[2:]
    outs, (state_ref, scaled_ref) = refs[: len(jobs)], refs[len(jobs) :]
    slab = slabs[0].shape[0]
    for i in range(4):
        state_ref[i * slab : (i + 1) * slab, :] = slabs[i][...]
    span = state_ref.shape[1]
    blocks = dense_ref.shape[0]
    deep = scaled_ref.shape[0] // blocks
    tall, depth = timed_ref.shape[2:]
    bands = tall // (2 * BAND)
    bands_in = bands // blocks
    row_block = bands_in * BAND
    owners, inner, targets = outs[0].shape[1], outs[0].shape[3], outs[0].shape[4]
    pair = 2 * targets

    for (half, first, count), out_ref in zip(jobs, outs):
        timed = timed_ref[half, first : first + count].reshape(count * tall, depth)

        def states(step, carry):
            columns = pl.ds(pl.multiple_of(step * pair, pair), pair)
            contracted = jnp.dot(timed, state_ref[:, columns], preferred_element_type=jnp.float32)
            gains = gains_ref[half, :, pl.ds(pl.multiple_of(part * span + step * pair, pair), pair)]
            for place in range(count):
                for time in range(2):
                    at = 2 * (first + place) + time
                    gain = gains[at : at + 1, :]
                    column = (2 * place + time) * targets
                    for band in range(bands):
                        row = place * tall + (2 * band + time) * BAND
                        block = (contracted[row : row + BAND, :] * gain).astype(jnp.bfloat16)
                        base = (band // bands_in) * deep + (band % bands_in) * BAND
                        for state in range(2):
                            start = pl.multiple_of(base + (step * 2 + state) * row_block, BAND)
                            scaled_ref[pl.ds(start, BAND), column : column + targets] = block[
                                :, state * targets : (state + 1) * targets
                            ]
            return carry

        lax.fori_loop(0, span // pair, states, 0)
        for place in range(count):
            columns = slice(place * pair, (place + 1) * pair)
            value = sum(
                jnp.dot(
                    dense_ref[block, :, part * deep : (part + 1) * deep],
                    scaled_ref[block * deep : (block + 1) * deep, columns],
                    preferred_element_type=jnp.float32,
                )
                for block in range(blocks)
            )
            for time in range(2):
                piece = value[:, time * targets : (time + 1) * targets].reshape(owners, inner, targets)
                if has_total:
                    piece = piece + totals[half][first + place, :, time, :, :]
                out_ref[place, :, time, :, :] = piece.astype(out_ref.dtype)


def contract(jobs, part, timed, gains, dense, slabs, totals, owners, dtypes):
    slab, span = slabs[0].shape
    rows = timed.shape[2] // 2
    states = dense.shape[0] * dense.shape[2] // rows
    targets = gains.shape[2] // states
    depth = span // targets * rows
    operands = [timed, gains, dense, *slabs, *totals]
    wide = max(count for _, _, count in jobs)
    work = sum(count for _, _, count in jobs)
    return pl.pallas_call(
        functools.partial(contract_kernel, jobs, part, bool(totals)),
        out_shape=[
            jax.ShapeDtypeStruct((count, owners, 2, dense.shape[1] // owners, targets), dtype)
            for (_, _, count), dtype in zip(jobs, dtypes)
        ],
        in_specs=[WHOLE] * len(operands),
        out_specs=[WHOLE] * len(jobs),
        scratch_shapes=[
            pltpu.VMEM((4 * slab, span), jnp.bfloat16),
            pltpu.VMEM((depth, wide * 2 * targets), jnp.bfloat16),
        ],
        compiler_params=params(),
        cost_estimate=pl.CostEstimate(
            flops=4 * work * (rows * 4 * slab * span + dense.shape[1] * depth * targets),
            bytes_accessed=2 * 1024 * 1024 * work,
            transcendentals=0,
        ),
    )(*operands)


def shards(
    screened, grid_weights, greens, three_state, three_orbital, block_ids, block_counts, owners
):
    freq_count = lax.axis_size("freq")
    aux_count = lax.axis_size("aux")
    freq = lax.axis_index("freq")
    chip, core = freq // 2, freq % 2
    local_times, rows, width = screened.shape
    total_times = local_times * freq_count
    states = three_state.shape[1]
    targets = three_state.shape[2]
    block_count, slot_count = block_ids.shape
    orbitals = three_orbital.shape[2]
    block_width = orbitals // slot_count
    row_block = rows // block_count
    chips = freq_count // 2
    height = aux_count // DEPTH

    along = []
    for f in range(freq_count):
        for y in range(height):
            for z in range(DEPTH):
                far = (z + SHIFTS[z % 2][f]) % DEPTH
                along.append((f * aux_count + y * DEPTH + far, f * aux_count + y * DEPTH + z))
    across = [
        [(((y + i) % height) * DEPTH + z, y * DEPTH + z) for y in range(height) for z in range(DEPTH)]
        for i in range(height)
    ]
    flat_state = three_state.reshape(rows, states * targets)
    flat_state, screened = lax.optimization_barrier((flat_state, screened))
    span = states * targets // 2
    parts = [flat_state[:, part * span : (part + 1) * span] for part in range(2)]
    own = lax.ppermute(parts[0], ("freq", "aux"), along)
    slabs = [[own] + [lax.ppermute(own, "aux", across[i]) for i in range(1, height)]]
    parts[1], slabs[0][0] = lax.optimization_barrier((parts[1], slabs[0][0]))
    own = lax.ppermute(parts[1], ("freq", "aux"), along)
    slabs.append([own])
    for i in range(1, height):
        ready, slabs[0][i] = lax.optimization_barrier((own, slabs[0][i]))
        slabs[1].append(lax.ppermute(ready, "aux", across[i]))

    place = lax.axis_index("aux").astype(jnp.int32).reshape(1)
    pieces = pick(place, screened, freq_count)
    pieces = lax.all_to_all(pieces, "freq", split_axis=0, concat_axis=0, tiled=True)

    half = jnp.arange(2, dtype=jnp.int32)[:, None, None]
    other = jnp.array(ORDER, dtype=jnp.int32)[None, :, None]
    step = jnp.arange(local_times, dtype=jnp.int32)[None, None, :]
    time = ((chip + other) % chips) * 2 * local_times + ((core + 1 + half) % 2) * local_times + step
    time = time.reshape(2, chips * local_times)
    freqs = jnp.arange(total_times, dtype=jnp.int32)
    lanes = jnp.arange(total_times * BAND, dtype=jnp.int32) // BAND
    weights = jnp.repeat(grid_weights, BAND)
    table = weights * jnp.cos(
        jnp.pi * (time[:, :, None].astype(jnp.float32) + 0.5) * lanes.astype(jnp.float32) / total_times
    )
    gains = jnp.sum(jnp.where(time[:, :, None, None] == freqs[:, None], greens, 0.0), axis=2)
    gains = jnp.repeat(gains, targets, axis=2)

    device = jnp.arange(aux_count, dtype=jnp.int32)
    owned = jnp.sum(jnp.where(owners[None, :] == device[:, None], device[None, :], 0), axis=1)
    inner = orbitals // aux_count
    wanted = (owned[:, None] * inner + jnp.arange(inner, dtype=jnp.int32)[None, :]).reshape(orbitals)
    slot = jnp.arange(slot_count, dtype=jnp.int32)
    listed = block_ids[:, :, None] * block_width + jnp.arange(block_width, dtype=jnp.int32)
    listed = jnp.where(slot[None, :, None] < block_counts[:, None, None], listed, -1).reshape(block_count, orbitals)
    choose = (wanted[None, :, None] == listed[:, None, :]).astype(jnp.bfloat16)
    _, three_orbital = lax.optimization_barrier((slabs[0][0], three_orbital))
    values = three_orbital.reshape(block_count, row_block, states, orbitals)
    values = values.transpose(0, 2, 1, 3).reshape(block_count, states * row_block, orbitals)
    dense = jnp.einsum("bns,brs->bnr", choose, values, preferred_element_type=jnp.float32).astype(jnp.bfloat16)

    slabs[0][1], pieces = lax.optimization_barrier((slabs[0][1], pieces))
    timed = transform(pieces, spread_table(table))
    run = functools.partial(contract, timed=timed, gains=gains, dense=dense, owners=aux_count)
    swap = [(f, f ^ 1) for f in range(freq_count)]
    totals = list(run(((0, 0, chips), (1, 0, chips)), 0, slabs=slabs[0], totals=[], dtypes=(jnp.float32,) * 2))

    def last(first, count, totals):
        jobs = ((0, first, count), (1, first, count))
        given, kept = run(jobs, 1, slabs=slabs[1], totals=totals, dtypes=(jnp.bfloat16, jnp.float32))
        taken = lax.ppermute(given, "freq", swap)
        return [kept[i] + taken[i].astype(jnp.float32) for i in range(count)]

    def send(value, by):
        moves = [(2 * x + c, 2 * ((x + by) % chips) + c) for x in range(chips) for c in range(2)]
        return lax.ppermute(value, "freq", moves)

    far = last(1, 1, totals)[0].astype(jnp.bfloat16)
    near = last(2, 2, totals)
    totals[0], far = lax.optimization_barrier((totals[0], far))
    arrived = [send(far, ORDER[1])] + [send(near[i].astype(jnp.bfloat16), ORDER[2 + i]) for i in range(2)]
    summed = last(0, 1, totals)[0]
    for piece in arrived:
        summed = summed + piece.astype(jnp.float32)
    spread = lax.all_to_all(summed.astype(jnp.bfloat16), "aux", split_axis=0, concat_axis=0, tiled=True)
    return jnp.sum(spread.astype(jnp.float32), axis=0)


def solution(mesh):
    return jax.shard_map(
        shards,
        mesh=mesh,
        in_specs=(
            P("freq", "aux", None),
            P(),
            P(),
            P("aux", None, None),
            P("aux", None, None),
            P("aux", None),
            P("aux"),
            P(),
        ),
        out_specs=P("freq", "aux", None),
        check_vma=False,
    )
```

```python
import functools

import jax
import jax.numpy as jnp
from jax import lax
from jax.experimental import pallas as pl
from jax.experimental.pallas import tpu as pltpu
from jax.sharding import PartitionSpec as P

BAND = 16
DEPTH = 8
SHIFTS = ((0, 4, 3, 5, 2, 6, 1, 7), (0, 4, 1, 7, 2, 6, 3, 5))
WHOLE = pl.BlockSpec(memory_space=pltpu.VMEM)


def params(mebibytes=32):
    return pltpu.CompilerParams(vmem_limit_bytes=mebibytes * 1024 * 1024)


def pick_kernel(place_ref, screened_ref, out_ref, piece_ref, sems):
    place = place_ref[0]
    row, column = place // DEPTH, place % DEPTH
    odd = column % 2
    slab = out_ref.shape[3] // 4
    copies = []
    for f in range(out_ref.shape[0]):
        far = lax.rem(column + jnp.where(odd == 1, SHIFTS[1][f], SHIFTS[0][f]), DEPTH)
        for i in range(4):
            start = (lax.rem(row + i, 4) * DEPTH + far) * slab
            piece_ref[f, :, :, i * slab : (i + 1) * slab] = screened_ref[:, :, pl.ds(pl.multiple_of(start, slab), slab)]
        copies.append(pltpu.make_async_copy(piece_ref.at[f], out_ref.at[f], sems.at[f]))
        copies[-1].start()
    for copy in copies:
        copy.wait()


def pick(place, screened, freqs):
    local, rows, width = screened.shape
    shape = (freqs, local, rows, width // freqs)
    return pl.pallas_call(
        pick_kernel,
        out_shape=jax.ShapeDtypeStruct(shape, screened.dtype),
        in_specs=[pl.BlockSpec(memory_space=pltpu.SMEM), WHOLE],
        out_specs=pl.BlockSpec(memory_space=pl.ANY),
        scratch_shapes=[pltpu.VMEM(shape, screened.dtype), pltpu.SemaphoreType.DMA((freqs,))],
        compiler_params=params(16),
    )(place, screened)


def spread_kernel(table_ref, out_ref):
    times, wide = table_ref.shape[1:]
    lane = lax.broadcasted_iota(jnp.int32, (BAND, wide), 1) % BAND
    keep = lane == lax.broadcasted_iota(jnp.int32, (BAND, wide), 0)
    tall = times * BAND
    for half in range(2):
        for time in range(times):
            value = jnp.where(keep, table_ref[half, time : time + 1, :], 0.0)
            upper = value.astype(jnp.bfloat16)
            lower = (value - upper.astype(jnp.float32)).astype(jnp.bfloat16)
            out_ref[half, time * BAND : (time + 1) * BAND, :] = upper
            out_ref[half, tall + time * BAND : tall + (time + 1) * BAND, :] = lower


def spread_table(table):
    _, times, wide = table.shape
    return pl.pallas_call(
        spread_kernel,
        out_shape=jax.ShapeDtypeStruct((2, 2 * times * BAND, wide), jnp.bfloat16),
        in_specs=[WHOLE],
        out_specs=WHOLE,
        compiler_params=params(),
    )(table)


def mix_kernel(pieces_in, mix_ref, out_ref, pieces_ref, sems):
    sources, local, rows, width = pieces_ref.shape
    copies = []
    for i in range(rows // (2 * BAND)):
        part = pl.ds(i * 2 * BAND, 2 * BAND)
        copies.append(pltpu.make_async_copy(pieces_in.at[:, :, part], pieces_ref.at[:, :, part], sems.at[i]))
        copies[-1].start()
    freqs = sources * local
    places = out_ref.shape[1]
    pair = 2 * BAND
    tall = places * pair
    mix = mix_ref[...].reshape(4 * tall, freqs * BAND)
    for band in range(rows // BAND):
        if band % 2 == 0:
            copies[band // 2].wait()
        piece = pieces_ref[:, :, band * BAND : (band + 1) * BAND, :].reshape(freqs * BAND, width)
        both = jnp.dot(mix, piece, preferred_element_type=jnp.float32)
        for half in range(2):
            upper = both[2 * half * tall : (2 * half + 1) * tall]
            lower = both[(2 * half + 1) * tall : (2 * half + 2) * tall]
            mixed = (upper + lower).astype(jnp.bfloat16)
            for place in range(places):
                out_ref[half, place, band * pair : (band + 1) * pair, :] = mixed[place * pair : (place + 1) * pair]


def transform(pieces, mix):
    sources, local, rows, width = pieces.shape
    times = mix.shape[1] // (2 * BAND)
    return pl.pallas_call(
        mix_kernel,
        out_shape=jax.ShapeDtypeStruct((2, times // 2, 2 * rows, width), jnp.bfloat16),
        in_specs=[pl.BlockSpec(memory_space=pl.ANY), WHOLE],
        out_specs=WHOLE,
        scratch_shapes=[pltpu.VMEM(pieces.shape, pieces.dtype), pltpu.SemaphoreType.DMA((rows // (2 * BAND),))],
        compiler_params=params(),
    )(pieces, mix)


def contract_kernel(jobs, part, has_total, *refs):
    timed_ref, gains_ref, dense_ref = refs[:3]
    slabs = refs[3:7]
    refs = refs[7:]
    totals = ()
    if has_total:
        totals, refs = refs[:1], refs[1:]
    outs, (state_ref, scaled_ref) = refs[: len(jobs)], refs[len(jobs) :]
    slab = slabs[0].shape[0]
    for i in range(4):
        state_ref[i * slab : (i + 1) * slab, :] = slabs[i][...]
    span = state_ref.shape[1]
    blocks = dense_ref.shape[0]
    deep = scaled_ref.shape[0] // blocks
    tall, depth = timed_ref.shape[2:]
    bands = tall // (2 * BAND)
    bands_in = bands // blocks
    row_block = bands_in * BAND
    owners, inner, targets = outs[0].shape[1], outs[0].shape[3], outs[0].shape[4]
    pair = 2 * targets

    for (half, first, count), out_ref in zip(jobs, outs):
        timed = timed_ref[half, first : first + count].reshape(count * tall, depth)

        def states(step, carry):
            columns = pl.ds(pl.multiple_of(step * pair, pair), pair)
            contracted = jnp.dot(timed, state_ref[:, columns], preferred_element_type=jnp.float32)
            gains = gains_ref[half, :, pl.ds(pl.multiple_of(part * span + step * pair, pair), pair)]
            for place in range(count):
                for time in range(2):
                    at = 2 * (first + place) + time
                    gain = gains[at : at + 1, :]
                    column = (2 * place + time) * targets
                    for band in range(bands):
                        row = place * tall + (2 * band + time) * BAND
                        block = (contracted[row : row + BAND, :] * gain).astype(jnp.bfloat16)
                        base = (band // bands_in) * deep + (band % bands_in) * BAND
                        for state in range(2):
                            start = pl.multiple_of(base + (step * 2 + state) * row_block, BAND)
                            scaled_ref[pl.ds(start, BAND), column : column + targets] = block[
                                :, state * targets : (state + 1) * targets
                            ]
            return carry

        lax.fori_loop(0, span // pair, states, 0)
        for place in range(count):
            columns = slice(place * pair, (place + 1) * pair)
            value = sum(
                jnp.dot(
                    dense_ref[block, :, part * deep : (part + 1) * deep],
                    scaled_ref[block * deep : (block + 1) * deep, columns],
                    preferred_element_type=jnp.float32,
                )
                for block in range(blocks)
            )
            for time in range(2):
                piece = value[:, time * targets : (time + 1) * targets].reshape(owners, inner, targets)
                if has_total:
                    piece = piece + totals[0][first + place, :, time, :, :]
                out_ref[place, :, time, :, :] = piece.astype(out_ref.dtype)


def contract(jobs, part, timed, gains, dense, slabs, totals, owners, dtypes):
    slab, span = slabs[0].shape
    rows = timed.shape[2] // 2
    states = dense.shape[0] * dense.shape[2] // rows
    targets = gains.shape[2] // states
    depth = span // targets * rows
    operands = [timed, gains, dense, *slabs, *totals]
    wide = max(count for _, _, count in jobs)
    work = sum(count for _, _, count in jobs)
    return pl.pallas_call(
        functools.partial(contract_kernel, jobs, part, bool(totals)),
        out_shape=[
            jax.ShapeDtypeStruct((count, owners, 2, dense.shape[1] // owners, targets), dtype)
            for (_, _, count), dtype in zip(jobs, dtypes)
        ],
        in_specs=[WHOLE] * len(operands),
        out_specs=[WHOLE] * len(jobs),
        scratch_shapes=[
            pltpu.VMEM((4 * slab, span), jnp.bfloat16),
            pltpu.VMEM((depth, wide * 2 * targets), jnp.bfloat16),
        ],
        compiler_params=params(),
        cost_estimate=pl.CostEstimate(
            flops=4 * work * (rows * 4 * slab * span + dense.shape[1] * depth * targets),
            bytes_accessed=2 * 1024 * 1024 * work,
            transcendentals=0,
        ),
    )(*operands)


def shards(
    screened, grid_weights, greens, three_state, three_orbital, block_ids, block_counts, owners
):
    freq_count = lax.axis_size("freq")
    aux_count = lax.axis_size("aux")
    freq = lax.axis_index("freq")
    chip, core = freq // 2, freq % 2
    local_times, rows, width = screened.shape
    total_times = local_times * freq_count
    states = three_state.shape[1]
    targets = three_state.shape[2]
    block_count, slot_count = block_ids.shape
    orbitals = three_orbital.shape[2]
    block_width = orbitals // slot_count
    row_block = rows // block_count
    chips = freq_count // 2
    height = aux_count // DEPTH

    along = []
    for f in range(freq_count):
        for y in range(height):
            for z in range(DEPTH):
                far = (z + SHIFTS[z % 2][f]) % DEPTH
                along.append((f * aux_count + y * DEPTH + far, f * aux_count + y * DEPTH + z))
    across = [
        [(((y + i) % height) * DEPTH + z, y * DEPTH + z) for y in range(height) for z in range(DEPTH)]
        for i in range(height)
    ]
    flat_state = three_state.reshape(rows, states * targets)
    flat_state, screened = lax.optimization_barrier((flat_state, screened))
    span = states * targets // 2
    parts = [flat_state[:, part * span : (part + 1) * span] for part in range(2)]
    own = lax.ppermute(parts[0], ("freq", "aux"), along)
    slabs = [[own] + [lax.ppermute(own, "aux", across[i]) for i in range(1, height)]]
    parts[1], slabs[0][0] = lax.optimization_barrier((parts[1], slabs[0][0]))
    own = lax.ppermute(parts[1], ("freq", "aux"), along)
    slabs.append([own])
    for i in range(1, height):
        ready, slabs[0][i] = lax.optimization_barrier((own, slabs[0][i]))
        slabs[1].append(lax.ppermute(ready, "aux", across[i]))

    place = lax.axis_index("aux").astype(jnp.int32).reshape(1)
    pieces = pick(place, screened, freq_count)
    pieces = lax.all_to_all(pieces, "freq", split_axis=0, concat_axis=0, tiled=True)

    half = jnp.arange(2, dtype=jnp.int32)[:, None, None]
    other = jnp.arange(chips, dtype=jnp.int32)[None, :, None]
    step = jnp.arange(local_times, dtype=jnp.int32)[None, None, :]
    time = ((chip + other) % chips) * 2 * local_times + ((core + 1 + half) % 2) * local_times + step
    time = time.reshape(2, chips * local_times)
    freqs = jnp.arange(total_times, dtype=jnp.int32)
    lanes = jnp.arange(total_times * BAND, dtype=jnp.int32) // BAND
    weights = jnp.repeat(grid_weights, BAND)
    table = weights * jnp.cos(
        jnp.pi * (time[:, :, None].astype(jnp.float32) + 0.5) * lanes.astype(jnp.float32) / total_times
    )
    gains = jnp.sum(jnp.where(time[:, :, None, None] == freqs[:, None], greens, 0.0), axis=2)
    gains = jnp.repeat(gains, targets, axis=2)

    device = jnp.arange(aux_count, dtype=jnp.int32)
    owned = jnp.sum(jnp.where(owners[None, :] == device[:, None], device[None, :], 0), axis=1)
    inner = orbitals // aux_count
    wanted = (owned[:, None] * inner + jnp.arange(inner, dtype=jnp.int32)[None, :]).reshape(orbitals)
    slot = jnp.arange(slot_count, dtype=jnp.int32)
    listed = block_ids[:, :, None] * block_width + jnp.arange(block_width, dtype=jnp.int32)
    listed = jnp.where(slot[None, :, None] < block_counts[:, None, None], listed, -1).reshape(block_count, orbitals)
    choose = (wanted[None, :, None] == listed[:, None, :]).astype(jnp.bfloat16)
    _, three_orbital = lax.optimization_barrier((slabs[0][1], three_orbital))
    values = three_orbital.reshape(block_count, row_block, states, orbitals)
    values = values.transpose(0, 2, 1, 3).reshape(block_count, states * row_block, orbitals)
    dense = jnp.einsum("bns,brs->bnr", choose, values, preferred_element_type=jnp.float32).astype(jnp.bfloat16)

    slabs[0][1], pieces = lax.optimization_barrier((slabs[0][1], pieces))
    timed = transform(pieces, spread_table(table))
    run = functools.partial(contract, timed=timed, gains=gains, dense=dense, owners=aux_count)
    swap = [(f, f ^ 1) for f in range(freq_count)]
    away = chips - 1
    totals = run(((0, 0, chips), (1, 0, chips)), 0, slabs=slabs[0], totals=[], dtypes=(jnp.float32,) * 2)
    (given,) = run(((0, 0, chips),), 1, slabs=slabs[1], totals=[totals[0]], dtypes=(jnp.bfloat16,))
    taken = lax.ppermute(given, "freq", swap)
    (kept,) = run(((1, 1, away),), 1, slabs=slabs[1], totals=[totals[1]], dtypes=(jnp.float32,))
    sent = [(kept[i - 1] + taken[i].astype(jnp.float32)).astype(jnp.bfloat16) for i in range(1, chips)]

    def chip_shift(by):
        return [(2 * x + c, 2 * ((x + by) % chips) + c) for x in range(chips) for c in range(2)]

    own, sent[0] = lax.optimization_barrier((totals[1], sent[0]))
    arrived = [lax.ppermute(sent[i], "freq", chip_shift(i + 1)) for i in range(away)]
    (kept,) = run(((1, 0, 1),), 1, slabs=slabs[1], totals=[own], dtypes=(jnp.float32,))
    summed = kept[0] + taken[0].astype(jnp.float32)
    for piece in arrived:
        summed = summed + piece.astype(jnp.float32)
    spread = lax.all_to_all(summed.astype(jnp.bfloat16), "aux", split_axis=0, concat_axis=0, tiled=True)
    return jnp.sum(spread.astype(jnp.float32), axis=0)


def solution(mesh):
    return jax.shard_map(
        shards,
        mesh=mesh,
        in_specs=(
            P("freq", "aux", None),
            P(),
            P(),
            P("aux", None, None),
            P("aux", None, None),
            P("aux", None),
            P("aux"),
            P(),
        ),
        out_specs=P("freq", "aux", None),
        check_vma=False,
    )
```

```python
import functools

import jax
import jax.numpy as jnp
from jax import lax
from jax.experimental import pallas as pl
from jax.experimental.pallas import tpu as pltpu
from jax.sharding import PartitionSpec as P

BAND = 16
DEPTH = 8
SHIFTS = ((0, 4, 3, 5, 2, 6, 1, 7), (0, 4, 1, 7, 2, 6, 3, 5))
WHOLE = pl.BlockSpec(memory_space=pltpu.VMEM)


def params(mebibytes=24):
    return pltpu.CompilerParams(vmem_limit_bytes=mebibytes * 1024 * 1024)


def pick_kernel(place_ref, screened_ref, out_ref, piece_ref, sems):
    place = place_ref[0]
    row, column = place // DEPTH, place % DEPTH
    odd = column % 2
    slab = out_ref.shape[3] // 4
    copies = []
    for f in range(out_ref.shape[0]):
        far = lax.rem(column + jnp.where(odd == 1, SHIFTS[1][f], SHIFTS[0][f]), DEPTH)
        for i in range(4):
            start = (lax.rem(row + i, 4) * DEPTH + far) * slab
            piece_ref[f, :, :, i * slab : (i + 1) * slab] = screened_ref[:, :, pl.ds(pl.multiple_of(start, slab), slab)]
        copies.append(pltpu.make_async_copy(piece_ref.at[f], out_ref.at[f], sems.at[f]))
        copies[-1].start()
    for copy in copies:
        copy.wait()


def pick(place, screened, freqs):
    local, rows, width = screened.shape
    shape = (freqs, local, rows, width // freqs)
    return pl.pallas_call(
        pick_kernel,
        out_shape=jax.ShapeDtypeStruct(shape, screened.dtype),
        in_specs=[pl.BlockSpec(memory_space=pltpu.SMEM), WHOLE],
        out_specs=pl.BlockSpec(memory_space=pl.ANY),
        scratch_shapes=[pltpu.VMEM(shape, screened.dtype), pltpu.SemaphoreType.DMA((freqs,))],
        compiler_params=params(8),
    )(place, screened)


def spread_kernel(table_ref, out_ref):
    times, wide = table_ref.shape[1:]
    lane = lax.broadcasted_iota(jnp.int32, (BAND, wide), 1) % BAND
    keep = lane == lax.broadcasted_iota(jnp.int32, (BAND, wide), 0)
    tall = times * BAND
    for half in range(2):
        for time in range(times):
            value = jnp.where(keep, table_ref[half, time : time + 1, :], 0.0)
            upper = value.astype(jnp.bfloat16)
            lower = (value - upper.astype(jnp.float32)).astype(jnp.bfloat16)
            out_ref[half, time * BAND : (time + 1) * BAND, :] = upper
            out_ref[half, tall + time * BAND : tall + (time + 1) * BAND, :] = lower


def spread_table(table):
    _, times, wide = table.shape
    return pl.pallas_call(
        spread_kernel,
        out_shape=jax.ShapeDtypeStruct((2, 2 * times * BAND, wide), jnp.bfloat16),
        in_specs=[WHOLE],
        out_specs=WHOLE,
        compiler_params=params(),
    )(table)


def mix_kernel(pieces_ref, mix_ref, out_ref):
    sources, local, rows, width = pieces_ref.shape
    freqs = sources * local
    places = out_ref.shape[1]
    pair = 2 * BAND
    tall = places * pair
    mix = mix_ref[...].reshape(4 * tall, freqs * BAND)
    for band in range(rows // BAND):
        piece = pieces_ref[:, :, band * BAND : (band + 1) * BAND, :].reshape(freqs * BAND, width)
        both = jnp.dot(mix, piece, preferred_element_type=jnp.float32)
        for half in range(2):
            upper = both[2 * half * tall : (2 * half + 1) * tall]
            lower = both[(2 * half + 1) * tall : (2 * half + 2) * tall]
            mixed = (upper + lower).astype(jnp.bfloat16)
            for place in range(places):
                out_ref[half, place, band * pair : (band + 1) * pair, :] = mixed[place * pair : (place + 1) * pair]


def transform(pieces, mix):
    sources, local, rows, width = pieces.shape
    times = mix.shape[1] // (2 * BAND)
    return pl.pallas_call(
        mix_kernel,
        out_shape=jax.ShapeDtypeStruct((2, times // 2, 2 * rows, width), jnp.bfloat16),
        in_specs=[WHOLE] * 2,
        out_specs=WHOLE,
        compiler_params=params(),
    )(pieces, mix)


def contract_kernel(jobs, part, has_total, *refs):
    timed_ref, gains_ref, dense_ref = refs[:3]
    slabs = refs[3:7]
    refs = refs[7:]
    totals = ()
    if has_total:
        totals, refs = refs[:1], refs[1:]
    outs, (state_ref, scaled_ref) = refs[: len(jobs)], refs[len(jobs) :]
    slab = slabs[0].shape[0]
    for i in range(4):
        state_ref[i * slab : (i + 1) * slab, :] = slabs[i][...]
    span = state_ref.shape[1]
    blocks = dense_ref.shape[0]
    deep = scaled_ref.shape[0] // blocks
    tall, depth = timed_ref.shape[2:]
    bands = tall // (2 * BAND)
    bands_in = bands // blocks
    row_block = bands_in * BAND
    owners, inner, targets = outs[0].shape[1], outs[0].shape[3], outs[0].shape[4]
    pair = 2 * targets

    for (half, first, count), out_ref in zip(jobs, outs):
        timed = timed_ref[half, first : first + count].reshape(count * tall, depth)

        def states(step, carry):
            columns = pl.ds(pl.multiple_of(step * pair, pair), pair)
            contracted = jnp.dot(timed, state_ref[:, columns], preferred_element_type=jnp.float32)
            gains = gains_ref[half, :, pl.ds(pl.multiple_of(part * span + step * pair, pair), pair)]
            for place in range(count):
                for time in range(2):
                    at = 2 * (first + place) + time
                    gain = gains[at : at + 1, :]
                    column = (2 * place + time) * targets
                    for band in range(bands):
                        row = place * tall + (2 * band + time) * BAND
                        block = (contracted[row : row + BAND, :] * gain).astype(jnp.bfloat16)
                        base = (band // bands_in) * deep + (band % bands_in) * BAND
                        for state in range(2):
                            start = pl.multiple_of(base + (step * 2 + state) * row_block, BAND)
                            scaled_ref[pl.ds(start, BAND), column : column + targets] = block[
                                :, state * targets : (state + 1) * targets
                            ]
            return carry

        lax.fori_loop(0, span // pair, states, 0)
        for place in range(count):
            columns = slice(place * pair, (place + 1) * pair)
            value = sum(
                jnp.dot(
                    dense_ref[block, :, part * deep : (part + 1) * deep],
                    scaled_ref[block * deep : (block + 1) * deep, columns],
                    preferred_element_type=jnp.float32,
                )
                for block in range(blocks)
            )
            for time in range(2):
                piece = value[:, time * targets : (time + 1) * targets].reshape(owners, inner, targets)
                if has_total:
                    piece = piece + totals[0][first + place, :, time, :, :]
                out_ref[place, :, time, :, :] = piece.astype(out_ref.dtype)


def contract(jobs, part, timed, gains, dense, slabs, totals, owners, dtypes):
    slab, span = slabs[0].shape
    rows = timed.shape[2] // 2
    states = dense.shape[0] * dense.shape[2] // rows
    targets = gains.shape[2] // states
    depth = span // targets * rows
    operands = [timed, gains, dense, *slabs, *totals]
    wide = max(count for _, _, count in jobs)
    work = sum(count for _, _, count in jobs)
    return pl.pallas_call(
        functools.partial(contract_kernel, jobs, part, bool(totals)),
        out_shape=[
            jax.ShapeDtypeStruct((count, owners, 2, dense.shape[1] // owners, targets), dtype)
            for (_, _, count), dtype in zip(jobs, dtypes)
        ],
        in_specs=[WHOLE] * len(operands),
        out_specs=[WHOLE] * len(jobs),
        scratch_shapes=[
            pltpu.VMEM((4 * slab, span), jnp.bfloat16),
            pltpu.VMEM((depth, wide * 2 * targets), jnp.bfloat16),
        ],
        compiler_params=params(),
        cost_estimate=pl.CostEstimate(
            flops=4 * work * (rows * 4 * slab * span + dense.shape[1] * depth * targets),
            bytes_accessed=2 * 1024 * 1024 * work,
            transcendentals=0,
        ),
    )(*operands)


def shards(
    screened, grid_weights, greens, three_state, three_orbital, block_ids, block_counts, owners
):
    freq_count = lax.axis_size("freq")
    aux_count = lax.axis_size("aux")
    freq = lax.axis_index("freq")
    chip, core = freq // 2, freq % 2
    local_times, rows, width = screened.shape
    total_times = local_times * freq_count
    states = three_state.shape[1]
    targets = three_state.shape[2]
    block_count, slot_count = block_ids.shape
    orbitals = three_orbital.shape[2]
    block_width = orbitals // slot_count
    row_block = rows // block_count
    chips = freq_count // 2
    height = aux_count // DEPTH

    along = []
    for f in range(freq_count):
        for y in range(height):
            for z in range(DEPTH):
                far = (z + SHIFTS[z % 2][f]) % DEPTH
                along.append((f * aux_count + y * DEPTH + far, f * aux_count + y * DEPTH + z))
    across = [
        [(((y + i) % height) * DEPTH + z, y * DEPTH + z) for y in range(height) for z in range(DEPTH)]
        for i in range(height)
    ]
    flat_state = three_state.reshape(rows, states * targets)
    flat_state, screened = lax.optimization_barrier((flat_state, screened))
    span = states * targets // 2
    parts = [flat_state[:, part * span : (part + 1) * span] for part in range(2)]
    own = lax.ppermute(parts[0], ("freq", "aux"), along)
    slabs = [[own] + [lax.ppermute(own, "aux", across[i]) for i in range(1, height)]]
    parts[1], slabs[0][0] = lax.optimization_barrier((parts[1], slabs[0][0]))
    own = lax.ppermute(parts[1], ("freq", "aux"), along)
    slabs.append([own])
    for i in range(1, height):
        ready, slabs[0][i] = lax.optimization_barrier((own, slabs[0][i]))
        slabs[1].append(lax.ppermute(ready, "aux", across[i]))

    place = lax.axis_index("aux").astype(jnp.int32).reshape(1)
    pieces = pick(place, screened, freq_count)
    pieces = lax.all_to_all(pieces, "freq", split_axis=0, concat_axis=0, tiled=True)

    half = jnp.arange(2, dtype=jnp.int32)[:, None, None]
    other = jnp.arange(chips, dtype=jnp.int32)[None, :, None]
    step = jnp.arange(local_times, dtype=jnp.int32)[None, None, :]
    time = ((chip + other) % chips) * 2 * local_times + ((core + 1 + half) % 2) * local_times + step
    time = time.reshape(2, chips * local_times)
    freqs = jnp.arange(total_times, dtype=jnp.int32)
    lanes = jnp.arange(total_times * BAND, dtype=jnp.int32) // BAND
    weights = jnp.repeat(grid_weights, BAND)
    table = weights * jnp.cos(
        jnp.pi * (time[:, :, None].astype(jnp.float32) + 0.5) * lanes.astype(jnp.float32) / total_times
    )
    gains = jnp.sum(jnp.where(time[:, :, None, None] == freqs[:, None], greens, 0.0), axis=2)
    gains = jnp.repeat(gains, targets, axis=2)

    device = jnp.arange(aux_count, dtype=jnp.int32)
    owned = jnp.sum(jnp.where(owners[None, :] == device[:, None], device[None, :], 0), axis=1)
    inner = orbitals // aux_count
    wanted = (owned[:, None] * inner + jnp.arange(inner, dtype=jnp.int32)[None, :]).reshape(orbitals)
    slot = jnp.arange(slot_count, dtype=jnp.int32)
    listed = block_ids[:, :, None] * block_width + jnp.arange(block_width, dtype=jnp.int32)
    listed = jnp.where(slot[None, :, None] < block_counts[:, None, None], listed, -1).reshape(block_count, orbitals)
    choose = (wanted[None, :, None] == listed[:, None, :]).astype(jnp.bfloat16)
    _, three_orbital = lax.optimization_barrier((slabs[0][0], three_orbital))
    values = three_orbital.reshape(block_count, row_block, states, orbitals)
    values = values.transpose(0, 2, 1, 3).reshape(block_count, states * row_block, orbitals)
    dense = jnp.einsum("bns,brs->bnr", choose, values, preferred_element_type=jnp.float32).astype(jnp.bfloat16)

    timed = transform(pieces, spread_table(table))
    run = functools.partial(contract, timed=timed, gains=gains, dense=dense, owners=aux_count)
    swap = [(f, f ^ 1) for f in range(freq_count)]
    away = chips - 1
    totals = run(((0, 0, chips), (1, 0, chips)), 0, slabs=slabs[0], totals=[], dtypes=(jnp.float32,) * 2)
    (given,) = run(((0, 0, chips),), 1, slabs=slabs[1], totals=[totals[0]], dtypes=(jnp.bfloat16,))
    taken = lax.ppermute(given, "freq", swap)
    (kept,) = run(((1, 1, away),), 1, slabs=slabs[1], totals=[totals[1]], dtypes=(jnp.float32,))
    sent = [(kept[i - 1] + taken[i].astype(jnp.float32)).astype(jnp.bfloat16) for i in range(1, chips)]

    def chip_shift(by):
        return [(2 * x + c, 2 * ((x + by) % chips) + c) for x in range(chips) for c in range(2)]

    own, sent[0] = lax.optimization_barrier((totals[1], sent[0]))
    arrived = [lax.ppermute(sent[i], "freq", chip_shift(i + 1)) for i in range(away)]
    (kept,) = run(((1, 0, 1),), 1, slabs=slabs[1], totals=[own], dtypes=(jnp.float32,))
    summed = kept[0] + taken[0].astype(jnp.float32)
    for piece in arrived:
        summed = summed + piece.astype(jnp.float32)
    spread = lax.all_to_all(summed.astype(jnp.bfloat16), "aux", split_axis=0, concat_axis=0, tiled=True)
    return jnp.sum(spread.astype(jnp.float32), axis=0)


def solution(mesh):
    return jax.shard_map(
        shards,
        mesh=mesh,
        in_specs=(
            P("freq", "aux", None),
            P(),
            P(),
            P("aux", None, None),
            P("aux", None, None),
            P("aux", None),
            P("aux"),
            P(),
        ),
        out_specs=P("freq", "aux", None),
        check_vma=False,
    )
```

```python
import functools

import jax
import jax.numpy as jnp
from jax import lax
from jax.experimental import pallas as pl
from jax.experimental.pallas import tpu as pltpu
from jax.sharding import PartitionSpec as P

BAND = 16
DEPTH = 8
SHIFTS = ((0, 4, 3, 5, 2, 6, 1, 7), (0, 4, 1, 7, 2, 6, 3, 5))
WHOLE = pl.BlockSpec(memory_space=pltpu.VMEM)


def params(mebibytes=24):
    return pltpu.CompilerParams(vmem_limit_bytes=mebibytes * 1024 * 1024)


def pick_kernel(place_ref, screened_ref, out_ref, piece_ref, sems):
    place = place_ref[0]
    row, column = place // DEPTH, place % DEPTH
    odd = column % 2
    slab = out_ref.shape[3] // 4
    copies = []
    for f in range(out_ref.shape[0]):
        far = lax.rem(column + jnp.where(odd == 1, SHIFTS[1][f], SHIFTS[0][f]), DEPTH)
        for i in range(4):
            start = (lax.rem(row + i, 4) * DEPTH + far) * slab
            piece_ref[f, :, :, i * slab : (i + 1) * slab] = screened_ref[:, :, pl.ds(pl.multiple_of(start, slab), slab)]
        copies.append(pltpu.make_async_copy(piece_ref.at[f], out_ref.at[f], sems.at[f]))
        copies[-1].start()
    for copy in copies:
        copy.wait()


def pick(place, screened, freqs):
    local, rows, width = screened.shape
    shape = (freqs, local, rows, width // freqs)
    return pl.pallas_call(
        pick_kernel,
        out_shape=jax.ShapeDtypeStruct(shape, screened.dtype),
        in_specs=[pl.BlockSpec(memory_space=pltpu.SMEM), WHOLE],
        out_specs=pl.BlockSpec(memory_space=pl.ANY),
        scratch_shapes=[pltpu.VMEM(shape, screened.dtype), pltpu.SemaphoreType.DMA((freqs,))],
        compiler_params=params(8),
    )(place, screened)


def spread_kernel(table_ref, out_ref):
    times, wide = table_ref.shape[1:]
    lane = lax.broadcasted_iota(jnp.int32, (BAND, wide), 1) % BAND
    keep = lane == lax.broadcasted_iota(jnp.int32, (BAND, wide), 0)
    tall = times * BAND
    for half in range(2):
        for time in range(times):
            value = jnp.where(keep, table_ref[half, time : time + 1, :], 0.0)
            upper = value.astype(jnp.bfloat16)
            lower = (value - upper.astype(jnp.float32)).astype(jnp.bfloat16)
            out_ref[half, time * BAND : (time + 1) * BAND, :] = upper
            out_ref[half, tall + time * BAND : tall + (time + 1) * BAND, :] = lower


def spread_table(table):
    _, times, wide = table.shape
    return pl.pallas_call(
        spread_kernel,
        out_shape=jax.ShapeDtypeStruct((2, 2 * times * BAND, wide), jnp.bfloat16),
        in_specs=[WHOLE],
        out_specs=WHOLE,
        compiler_params=params(),
    )(table)


def mix_kernel(pieces_ref, mix_ref, out_ref):
    sources, local, rows, width = pieces_ref.shape
    freqs = sources * local
    places = out_ref.shape[1]
    pair = 2 * BAND
    tall = places * pair
    mix = mix_ref[...].reshape(4 * tall, freqs * BAND)
    for band in range(rows // BAND):
        piece = pieces_ref[:, :, band * BAND : (band + 1) * BAND, :].reshape(freqs * BAND, width)
        both = jnp.dot(mix, piece, preferred_element_type=jnp.float32)
        for half in range(2):
            upper = both[2 * half * tall : (2 * half + 1) * tall]
            lower = both[(2 * half + 1) * tall : (2 * half + 2) * tall]
            mixed = (upper + lower).astype(jnp.bfloat16)
            for place in range(places):
                out_ref[half, place, band * pair : (band + 1) * pair, :] = mixed[place * pair : (place + 1) * pair]


def transform(pieces, mix):
    sources, local, rows, width = pieces.shape
    times = mix.shape[1] // (2 * BAND)
    return pl.pallas_call(
        mix_kernel,
        out_shape=jax.ShapeDtypeStruct((2, times // 2, 2 * rows, width), jnp.bfloat16),
        in_specs=[WHOLE] * 2,
        out_specs=WHOLE,
        compiler_params=params(),
    )(pieces, mix)


def contract_kernel(jobs, part, has_total, *refs):
    timed_ref, gains_ref, dense_ref = refs[:3]
    slabs = refs[3:7]
    refs = refs[7:]
    totals = ()
    if has_total:
        totals, refs = refs[:1], refs[1:]
    outs, (state_ref, scaled_ref) = refs[: len(jobs)], refs[len(jobs) :]
    slab = slabs[0].shape[0]
    for i in range(4):
        state_ref[i * slab : (i + 1) * slab, :] = slabs[i][...]
    span = state_ref.shape[1]
    blocks = dense_ref.shape[0]
    deep = scaled_ref.shape[0] // blocks
    tall, depth = timed_ref.shape[2:]
    bands = tall // (2 * BAND)
    bands_in = bands // blocks
    row_block = bands_in * BAND
    owners, inner, targets = outs[0].shape[1], outs[0].shape[3], outs[0].shape[4]
    pair = 2 * targets

    for (half, first, count), out_ref in zip(jobs, outs):
        timed = timed_ref[half, first : first + count].reshape(count * tall, depth)

        def states(step, carry):
            columns = pl.ds(pl.multiple_of(step * pair, pair), pair)
            contracted = jnp.dot(timed, state_ref[:, columns], preferred_element_type=jnp.float32)
            gains = gains_ref[half, :, pl.ds(pl.multiple_of(part * span + step * pair, pair), pair)]
            for place in range(count):
                for time in range(2):
                    at = 2 * (first + place) + time
                    gain = gains[at : at + 1, :]
                    column = (2 * place + time) * targets
                    for band in range(bands):
                        row = place * tall + (2 * band + time) * BAND
                        block = (contracted[row : row + BAND, :] * gain).astype(jnp.bfloat16)
                        base = (band // bands_in) * deep + (band % bands_in) * BAND
                        for state in range(2):
                            start = pl.multiple_of(base + (step * 2 + state) * row_block, BAND)
                            scaled_ref[pl.ds(start, BAND), column : column + targets] = block[
                                :, state * targets : (state + 1) * targets
                            ]
            return carry

        lax.fori_loop(0, span // pair, states, 0)
        for place in range(count):
            columns = slice(place * pair, (place + 1) * pair)
            value = sum(
                jnp.dot(
                    dense_ref[block, :, part * deep : (part + 1) * deep],
                    scaled_ref[block * deep : (block + 1) * deep, columns],
                    preferred_element_type=jnp.float32,
                )
                for block in range(blocks)
            )
            for time in range(2):
                piece = value[:, time * targets : (time + 1) * targets].reshape(owners, inner, targets)
                if has_total:
                    piece = piece + totals[0][first + place, :, time, :, :]
                out_ref[place, :, time, :, :] = piece.astype(out_ref.dtype)


def contract(jobs, part, timed, gains, dense, slabs, totals, owners, dtypes):
    slab, span = slabs[0].shape
    rows = timed.shape[2] // 2
    states = dense.shape[0] * dense.shape[2] // rows
    targets = gains.shape[2] // states
    depth = span // targets * rows
    operands = [timed, gains, dense, *slabs, *totals]
    wide = max(count for _, _, count in jobs)
    work = sum(count for _, _, count in jobs)
    return pl.pallas_call(
        functools.partial(contract_kernel, jobs, part, bool(totals)),
        out_shape=[
            jax.ShapeDtypeStruct((count, owners, 2, dense.shape[1] // owners, targets), dtype)
            for (_, _, count), dtype in zip(jobs, dtypes)
        ],
        in_specs=[WHOLE] * len(operands),
        out_specs=[WHOLE] * len(jobs),
        scratch_shapes=[
            pltpu.VMEM((4 * slab, span), jnp.bfloat16),
            pltpu.VMEM((depth, wide * 2 * targets), jnp.bfloat16),
        ],
        compiler_params=params(),
        cost_estimate=pl.CostEstimate(
            flops=4 * work * (rows * 4 * slab * span + dense.shape[1] * depth * targets),
            bytes_accessed=2 * 1024 * 1024 * work,
            transcendentals=0,
        ),
    )(*operands)


def shards(
    screened, grid_weights, greens, three_state, three_orbital, block_ids, block_counts, owners
):
    freq_count = lax.axis_size("freq")
    aux_count = lax.axis_size("aux")
    freq = lax.axis_index("freq")
    chip, core = freq // 2, freq % 2
    local_times, rows, width = screened.shape
    total_times = local_times * freq_count
    states = three_state.shape[1]
    targets = three_state.shape[2]
    block_count, slot_count = block_ids.shape
    orbitals = three_orbital.shape[2]
    block_width = orbitals // slot_count
    row_block = rows // block_count
    chips = freq_count // 2
    height = aux_count // DEPTH

    along = []
    for f in range(freq_count):
        for y in range(height):
            for z in range(DEPTH):
                far = (z + SHIFTS[z % 2][f]) % DEPTH
                along.append((f * aux_count + y * DEPTH + far, f * aux_count + y * DEPTH + z))
    across = [
        [(((y + i) % height) * DEPTH + z, y * DEPTH + z) for y in range(height) for z in range(DEPTH)]
        for i in range(height)
    ]
    flat_state = three_state.reshape(rows, states * targets)
    flat_state, screened = lax.optimization_barrier((flat_state, screened))
    span = states * targets // 2
    parts = jnp.stack([flat_state[:, part * span : (part + 1) * span] for part in range(2)])
    own = lax.ppermute(parts, ("freq", "aux"), along)
    slabs = [[own[0]] + [lax.ppermute(own[0], "aux", across[i]) for i in range(1, height)], [own[1]]]
    for i in range(1, height):
        ready, slabs[0][i] = lax.optimization_barrier((own[1], slabs[0][i]))
        slabs[1].append(lax.ppermute(ready, "aux", across[i]))

    place = lax.axis_index("aux").astype(jnp.int32).reshape(1)
    pieces = pick(place, screened, freq_count)
    pieces = lax.all_to_all(pieces, "freq", split_axis=0, concat_axis=0, tiled=True)

    half = jnp.arange(2, dtype=jnp.int32)[:, None, None]
    other = jnp.arange(chips, dtype=jnp.int32)[None, :, None]
    step = jnp.arange(local_times, dtype=jnp.int32)[None, None, :]
    time = ((chip + other) % chips) * 2 * local_times + ((core + 1 + half) % 2) * local_times + step
    time = time.reshape(2, chips * local_times)
    freqs = jnp.arange(total_times, dtype=jnp.int32)
    lanes = jnp.arange(total_times * BAND, dtype=jnp.int32) // BAND
    weights = jnp.repeat(grid_weights, BAND)
    table = weights * jnp.cos(
        jnp.pi * (time[:, :, None].astype(jnp.float32) + 0.5) * lanes.astype(jnp.float32) / total_times
    )
    gains = jnp.sum(jnp.where(time[:, :, None, None] == freqs[:, None], greens, 0.0), axis=2)
    gains = jnp.repeat(gains, targets, axis=2)

    device = jnp.arange(aux_count, dtype=jnp.int32)
    owned = jnp.sum(jnp.where(owners[None, :] == device[:, None], device[None, :], 0), axis=1)
    inner = orbitals // aux_count
    wanted = (owned[:, None] * inner + jnp.arange(inner, dtype=jnp.int32)[None, :]).reshape(orbitals)
    slot = jnp.arange(slot_count, dtype=jnp.int32)
    listed = block_ids[:, :, None] * block_width + jnp.arange(block_width, dtype=jnp.int32)
    listed = jnp.where(slot[None, :, None] < block_counts[:, None, None], listed, -1).reshape(block_count, orbitals)
    choose = (wanted[None, :, None] == listed[:, None, :]).astype(jnp.bfloat16)
    _, three_orbital = lax.optimization_barrier((slabs[0][0], three_orbital))
    values = three_orbital.reshape(block_count, row_block, states, orbitals)
    values = values.transpose(0, 2, 1, 3).reshape(block_count, states * row_block, orbitals)
    dense = jnp.einsum("bns,brs->bnr", choose, values, preferred_element_type=jnp.float32).astype(jnp.bfloat16)

    timed = transform(pieces, spread_table(table))
    run = functools.partial(contract, timed=timed, gains=gains, dense=dense, owners=aux_count)
    swap = [(f, f ^ 1) for f in range(freq_count)]
    away = chips - 1
    totals = run(((0, 0, chips), (1, 0, chips)), 0, slabs=slabs[0], totals=[], dtypes=(jnp.float32,) * 2)
    (given,) = run(((0, 0, chips),), 1, slabs=slabs[1], totals=[totals[0]], dtypes=(jnp.bfloat16,))
    taken = lax.ppermute(given, "freq", swap)
    (kept,) = run(((1, 1, away),), 1, slabs=slabs[1], totals=[totals[1]], dtypes=(jnp.float32,))
    sent = [(kept[i - 1] + taken[i].astype(jnp.float32)).astype(jnp.bfloat16) for i in range(1, chips)]

    def chip_shift(by):
        return [(2 * x + c, 2 * ((x + by) % chips) + c) for x in range(chips) for c in range(2)]

    own, sent[0] = lax.optimization_barrier((totals[1], sent[0]))
    arrived = [lax.ppermute(sent[i], "freq", chip_shift(i + 1)) for i in range(away)]
    (kept,) = run(((1, 0, 1),), 1, slabs=slabs[1], totals=[own], dtypes=(jnp.float32,))
    summed = kept[0] + taken[0].astype(jnp.float32)
    for piece in arrived:
        summed = summed + piece.astype(jnp.float32)
    spread = lax.all_to_all(summed.astype(jnp.bfloat16), "aux", split_axis=0, concat_axis=0, tiled=True)
    return jnp.sum(spread.astype(jnp.float32), axis=0)


def solution(mesh):
    return jax.shard_map(
        shards,
        mesh=mesh,
        in_specs=(
            P("freq", "aux", None),
            P(),
            P(),
            P("aux", None, None),
            P("aux", None, None),
            P("aux", None),
            P("aux"),
            P(),
        ),
        out_specs=P("freq", "aux", None),
        check_vma=False,
    )
```

```python
import functools

import jax
import jax.numpy as jnp
from jax import lax
from jax.experimental import pallas as pl
from jax.experimental.pallas import tpu as pltpu
from jax.sharding import PartitionSpec as P

BAND = 16
DEPTH = 8
SHIFTS = ((0, 4, 3, 5, 2, 6, 1, 7), (0, 4, 1, 7, 2, 6, 3, 5))
WHOLE = pl.BlockSpec(memory_space=pltpu.VMEM)


def params(mebibytes=24):
    return pltpu.CompilerParams(vmem_limit_bytes=mebibytes * 1024 * 1024)


def pick_kernel(place_ref, screened_ref, out_ref, piece_ref, sems):
    place = place_ref[0]
    row, column = place // DEPTH, place % DEPTH
    odd = column % 2
    slab = out_ref.shape[3] // 4
    copies = []
    for f in range(out_ref.shape[0]):
        far = lax.rem(column + jnp.where(odd == 1, SHIFTS[1][f], SHIFTS[0][f]), DEPTH)
        for i in range(4):
            start = (lax.rem(row + i, 4) * DEPTH + far) * slab
            piece_ref[f, :, :, i * slab : (i + 1) * slab] = screened_ref[:, :, pl.ds(pl.multiple_of(start, slab), slab)]
        copies.append(pltpu.make_async_copy(piece_ref.at[f], out_ref.at[f], sems.at[f]))
        copies[-1].start()
    for copy in copies:
        copy.wait()


def pick(place, screened, freqs):
    local, rows, width = screened.shape
    shape = (freqs, local, rows, width // freqs)
    return pl.pallas_call(
        pick_kernel,
        out_shape=jax.ShapeDtypeStruct(shape, screened.dtype),
        in_specs=[pl.BlockSpec(memory_space=pltpu.SMEM), WHOLE],
        out_specs=pl.BlockSpec(memory_space=pl.ANY),
        scratch_shapes=[pltpu.VMEM(shape, screened.dtype), pltpu.SemaphoreType.DMA((freqs,))],
        compiler_params=params(8),
    )(place, screened)


def spread_kernel(table_ref, out_ref):
    times, wide = table_ref.shape[1:]
    lane = lax.broadcasted_iota(jnp.int32, (BAND, wide), 1) % BAND
    keep = lane == lax.broadcasted_iota(jnp.int32, (BAND, wide), 0)
    tall = times * BAND
    for half in range(2):
        for time in range(times):
            value = jnp.where(keep, table_ref[half, time : time + 1, :], 0.0)
            upper = value.astype(jnp.bfloat16)
            lower = (value - upper.astype(jnp.float32)).astype(jnp.bfloat16)
            out_ref[half, time * BAND : (time + 1) * BAND, :] = upper
            out_ref[half, tall + time * BAND : tall + (time + 1) * BAND, :] = lower


def spread_table(table):
    _, times, wide = table.shape
    return pl.pallas_call(
        spread_kernel,
        out_shape=jax.ShapeDtypeStruct((2, 2 * times * BAND, wide), jnp.bfloat16),
        in_specs=[WHOLE],
        out_specs=WHOLE,
        compiler_params=params(),
    )(table)


def mix_kernel(pieces_ref, mix_ref, out_ref):
    sources, local, rows, width = pieces_ref.shape
    freqs = sources * local
    places = out_ref.shape[1]
    pair = 2 * BAND
    tall = places * pair
    mix = mix_ref[...].reshape(4 * tall, freqs * BAND)
    for band in range(rows // BAND):
        piece = pieces_ref[:, :, band * BAND : (band + 1) * BAND, :].reshape(freqs * BAND, width)
        both = jnp.dot(mix, piece, preferred_element_type=jnp.float32)
        for half in range(2):
            upper = both[2 * half * tall : (2 * half + 1) * tall]
            lower = both[(2 * half + 1) * tall : (2 * half + 2) * tall]
            mixed = (upper + lower).astype(jnp.bfloat16)
            for place in range(places):
                out_ref[half, place, band * pair : (band + 1) * pair, :] = mixed[place * pair : (place + 1) * pair]


def transform(pieces, mix):
    sources, local, rows, width = pieces.shape
    times = mix.shape[1] // (2 * BAND)
    return pl.pallas_call(
        mix_kernel,
        out_shape=jax.ShapeDtypeStruct((2, times // 2, 2 * rows, width), jnp.bfloat16),
        in_specs=[WHOLE] * 2,
        out_specs=WHOLE,
        compiler_params=params(),
    )(pieces, mix)


def contract_kernel(jobs, part, has_total, *refs):
    timed_ref, gains_ref, dense_ref = refs[:3]
    slabs = refs[3:7]
    refs = refs[7:]
    totals = ()
    if has_total:
        totals, refs = refs[:1], refs[1:]
    outs, (state_ref, scaled_ref) = refs[: len(jobs)], refs[len(jobs) :]
    slab = slabs[0].shape[0]
    for i in range(4):
        state_ref[i * slab : (i + 1) * slab, :] = slabs[i][...]
    span = state_ref.shape[1]
    blocks = dense_ref.shape[0]
    deep = scaled_ref.shape[0] // blocks
    tall, depth = timed_ref.shape[2:]
    bands = tall // (2 * BAND)
    bands_in = bands // blocks
    row_block = bands_in * BAND
    owners, inner, targets = outs[0].shape[1], outs[0].shape[3], outs[0].shape[4]
    pair = 2 * targets

    for (half, first, count), out_ref in zip(jobs, outs):
        timed = timed_ref[half, first : first + count].reshape(count * tall, depth)

        def states(step, carry):
            columns = pl.ds(pl.multiple_of(step * pair, pair), pair)
            contracted = jnp.dot(timed, state_ref[:, columns], preferred_element_type=jnp.float32)
            gains = gains_ref[half, :, pl.ds(pl.multiple_of(part * span + step * pair, pair), pair)]
            for place in range(count):
                for time in range(2):
                    at = 2 * (first + place) + time
                    gain = gains[at : at + 1, :]
                    column = (2 * place + time) * targets
                    for band in range(bands):
                        row = place * tall + (2 * band + time) * BAND
                        block = (contracted[row : row + BAND, :] * gain).astype(jnp.bfloat16)
                        base = (band // bands_in) * deep + (band % bands_in) * BAND
                        for state in range(2):
                            start = pl.multiple_of(base + (step * 2 + state) * row_block, BAND)
                            scaled_ref[pl.ds(start, BAND), column : column + targets] = block[
                                :, state * targets : (state + 1) * targets
                            ]
            return carry

        lax.fori_loop(0, span // pair, states, 0)
        for place in range(count):
            columns = slice(place * pair, (place + 1) * pair)
            value = sum(
                jnp.dot(
                    dense_ref[block, :, part * deep : (part + 1) * deep],
                    scaled_ref[block * deep : (block + 1) * deep, columns],
                    preferred_element_type=jnp.float32,
                )
                for block in range(blocks)
            )
            for time in range(2):
                piece = value[:, time * targets : (time + 1) * targets].reshape(owners, inner, targets)
                if has_total:
                    piece = piece + totals[0][first + place, :, time, :, :]
                out_ref[place, :, time, :, :] = piece.astype(out_ref.dtype)


def contract(jobs, part, timed, gains, dense, slabs, totals, owners, dtypes):
    slab, span = slabs[0].shape
    rows = timed.shape[2] // 2
    states = dense.shape[0] * dense.shape[2] // rows
    targets = gains.shape[2] // states
    depth = span // targets * rows
    operands = [timed, gains, dense, *slabs, *totals]
    wide = max(count for _, _, count in jobs)
    work = sum(count for _, _, count in jobs)
    return pl.pallas_call(
        functools.partial(contract_kernel, jobs, part, bool(totals)),
        out_shape=[
            jax.ShapeDtypeStruct((count, owners, 2, dense.shape[1] // owners, targets), dtype)
            for (_, _, count), dtype in zip(jobs, dtypes)
        ],
        in_specs=[WHOLE] * len(operands),
        out_specs=[WHOLE] * len(jobs),
        scratch_shapes=[
            pltpu.VMEM((4 * slab, span), jnp.bfloat16),
            pltpu.VMEM((depth, wide * 2 * targets), jnp.bfloat16),
        ],
        compiler_params=params(),
        cost_estimate=pl.CostEstimate(
            flops=4 * work * (rows * 4 * slab * span + dense.shape[1] * depth * targets),
            bytes_accessed=2 * 1024 * 1024 * work,
            transcendentals=0,
        ),
    )(*operands)


def shards(
    screened, grid_weights, greens, three_state, three_orbital, block_ids, block_counts, owners
):
    freq_count = lax.axis_size("freq")
    aux_count = lax.axis_size("aux")
    freq = lax.axis_index("freq")
    chip, core = freq // 2, freq % 2
    local_times, rows, width = screened.shape
    total_times = local_times * freq_count
    states = three_state.shape[1]
    targets = three_state.shape[2]
    block_count, slot_count = block_ids.shape
    orbitals = three_orbital.shape[2]
    block_width = orbitals // slot_count
    row_block = rows // block_count
    chips = freq_count // 2
    height = aux_count // DEPTH

    along = []
    for f in range(freq_count):
        for y in range(height):
            for z in range(DEPTH):
                far = (z + SHIFTS[z % 2][f]) % DEPTH
                along.append((f * aux_count + y * DEPTH + far, f * aux_count + y * DEPTH + z))
    across = [
        [(((y + i) % height) * DEPTH + z, y * DEPTH + z) for y in range(height) for z in range(DEPTH)]
        for i in range(height)
    ]
    span = states * targets // 2
    moved = lax.ppermute(three_state, ("freq", "aux"), along).reshape(rows, states * targets)
    own = [moved[:, part * span : (part + 1) * span] for part in range(2)]
    slabs = [[own[0]] + [lax.ppermute(own[0], "aux", across[i]) for i in range(1, height)], [own[1]]]
    for i in range(1, height):
        ready, slabs[0][i] = lax.optimization_barrier((own[1], slabs[0][i]))
        slabs[1].append(lax.ppermute(ready, "aux", across[i]))

    place = lax.axis_index("aux").astype(jnp.int32).reshape(1)
    pieces = pick(place, screened, freq_count)
    pieces = lax.all_to_all(pieces, "freq", split_axis=0, concat_axis=0, tiled=True)

    half = jnp.arange(2, dtype=jnp.int32)[:, None, None]
    other = jnp.arange(chips, dtype=jnp.int32)[None, :, None]
    step = jnp.arange(local_times, dtype=jnp.int32)[None, None, :]
    time = ((chip + other) % chips) * 2 * local_times + ((core + 1 + half) % 2) * local_times + step
    time = time.reshape(2, chips * local_times)
    freqs = jnp.arange(total_times, dtype=jnp.int32)
    lanes = jnp.arange(total_times * BAND, dtype=jnp.int32) // BAND
    weights = jnp.repeat(grid_weights, BAND)
    table = weights * jnp.cos(
        jnp.pi * (time[:, :, None].astype(jnp.float32) + 0.5) * lanes.astype(jnp.float32) / total_times
    )
    gains = jnp.sum(jnp.where(time[:, :, None, None] == freqs[:, None], greens, 0.0), axis=2)
    gains = jnp.repeat(gains, targets, axis=2)

    device = jnp.arange(aux_count, dtype=jnp.int32)
    owned = jnp.sum(jnp.where(owners[None, :] == device[:, None], device[None, :], 0), axis=1)
    inner = orbitals // aux_count
    wanted = (owned[:, None] * inner + jnp.arange(inner, dtype=jnp.int32)[None, :]).reshape(orbitals)
    slot = jnp.arange(slot_count, dtype=jnp.int32)
    listed = block_ids[:, :, None] * block_width + jnp.arange(block_width, dtype=jnp.int32)
    listed = jnp.where(slot[None, :, None] < block_counts[:, None, None], listed, -1).reshape(block_count, orbitals)
    choose = (wanted[None, :, None] == listed[:, None, :]).astype(jnp.bfloat16)
    _, three_orbital = lax.optimization_barrier((slabs[0][0], three_orbital))
    values = three_orbital.reshape(block_count, row_block, states, orbitals)
    values = values.transpose(0, 2, 1, 3).reshape(block_count, states * row_block, orbitals)
    dense = jnp.einsum("bns,brs->bnr", choose, values, preferred_element_type=jnp.float32).astype(jnp.bfloat16)

    timed = transform(pieces, spread_table(table))
    run = functools.partial(contract, timed=timed, gains=gains, dense=dense, owners=aux_count)
    swap = [(f, f ^ 1) for f in range(freq_count)]
    away = chips - 1
    totals = run(((0, 0, chips), (1, 0, chips)), 0, slabs=slabs[0], totals=[], dtypes=(jnp.float32,) * 2)
    (given,) = run(((0, 0, chips),), 1, slabs=slabs[1], totals=[totals[0]], dtypes=(jnp.bfloat16,))
    taken = lax.ppermute(given, "freq", swap)
    (kept,) = run(((1, 1, away),), 1, slabs=slabs[1], totals=[totals[1]], dtypes=(jnp.float32,))
    sent = [(kept[i - 1] + taken[i].astype(jnp.float32)).astype(jnp.bfloat16) for i in range(1, chips)]

    def chip_shift(by):
        return [(2 * x + c, 2 * ((x + by) % chips) + c) for x in range(chips) for c in range(2)]

    own, sent[0] = lax.optimization_barrier((totals[1], sent[0]))
    arrived = [lax.ppermute(sent[i], "freq", chip_shift(i + 1)) for i in range(away)]
    (kept,) = run(((1, 0, 1),), 1, slabs=slabs[1], totals=[own], dtypes=(jnp.float32,))
    summed = kept[0] + taken[0].astype(jnp.float32)
    for piece in arrived:
        summed = summed + piece.astype(jnp.float32)
    spread = lax.all_to_all(summed.astype(jnp.bfloat16), "aux", split_axis=0, concat_axis=0, tiled=True)
    return jnp.sum(spread.astype(jnp.float32), axis=0)


def solution(mesh):
    return jax.shard_map(
        shards,
        mesh=mesh,
        in_specs=(
            P("freq", "aux", None),
            P(),
            P(),
            P("aux", None, None),
            P("aux", None, None),
            P("aux", None),
            P("aux"),
            P(),
        ),
        out_specs=P("freq", "aux", None),
        check_vma=False,
    )
```
